32 devices in a mesh: context: 4 (over y, x), expert: 8 (over z, core).
Axes of the slice: x: 2, y: 2, z: 4, core: 2. Of those that a mesh axis runs over, the one named last changes fastest.
Arguments:
- queries: bfloat16 [64, 3072], P(None, 'expert'), may hold values from -14 to 14
- key_lift: bfloat16 [16, 128, 512], P('expert'), may hold values from -0.5 to 0.5
- value_lift: bfloat16 [16, 512, 128], P('expert'), may hold values from -0.25 to 0.25
- page_pool: bfloat16 [16, 64, 576], P('context'), may hold values from -6 to 6
- fresh_latents: bfloat16 [8, 8, 576], P('context'), may hold values from -6 to 6
- page_table: int32 [8, 12], replicated, may hold values from 0 to 15, as said below
- context_lengths: int32 [8], replicated, may hold values from 705 to 768, as said below
- tree_parents: int32 [8, 8], replicated, may hold values from -1 to 6, as said below
- out_weight: bfloat16 [2048, 7168], P('expert', 'context'), may hold values from -0.5 to 0.5
- residual: bfloat16 [64, 7168], P('expert', 'context'), may hold values from -6 to 6
- norm_gain: float32 [7168], replicated, may hold values from 0.5 to 2
- expert_ids: int32 [64, 8], P('expert'), may hold values from 0 to 7, all different within a row; in each aligned block of 8 rows (0 to 7, 8 to 15, ...) at most 8 rows name the same one
- route_weights: float32 [64, 8], P('expert'), may hold values from 0.1 to 0.6
- gate_matrix: bfloat16 [8, 7168, 1024], P('expert', None, 'context'), may hold values from -0.0625 to 0.0625
- up_matrix: bfloat16 [8, 7168, 1024], P('expert', None, 'context'), may hold values from -0.0625 to 0.0625
- down_matrix: bfloat16 [8, 1024, 7168], P('expert', 'context'), may hold values from -0.1875 to 0.1875
Outputs:
- layer_out: bfloat16 [64, 7168], P('expert', 'context')
The draws below stay inside these ranges and needn't reach their ends.
Inputs may be any that keep to these rules, and one draw needn't show every extreme that they name: `page_table`: the 12 pages of a leaf are distinct. `context_lengths`: entry k of a leaf's page table holds its context tokens k * 64 to k * 64 + 63; some leaf fills all 12 pages. `tree_parents`: token 0 of a leaf has parent -1; token t > 0 has a parent among tokens 0 to t - 1 of the same leaf. `expert_ids`: within each aligned block of 8 rows, no expert is named by more than 8 rows, a bound that some block reaches.
All inputs are finite; a program needn't handle non-finite values.
Results may differ from the reference program's by a relative error of at most 0.011.
Values may be sent and summed in bfloat16 or wider, within the bound.
A program may use at most 64 MiB of HBM per device.

```python
import math
import jax
import jax.numpy as jnp
import numpy as np
from jax import lax

D = 7168
LAT = 512
ROPE = 64
QK = 128
VD = 128
FFE = 1024
TOPK = 8
LOOK = 8
PAGE = 64
MAXP = 12
ROW_DEV = 8
HEADS = 16
EXPERTS = 8
CKV = 576
ROWS = 64
LEAVES = 8
POOL = 16
CAP = 8


def draw_queries(key, part):
    full_shape = (ROWS, HEADS, QK + ROPE)
    sample = jnp.clip(jax.random.normal(jax.random.fold_in(key, 12), full_shape, jnp.float32), -6.0, 6.0)
    return sample.reshape(ROWS, HEADS * (QK + ROPE)).astype(jnp.bfloat16)


def draw_page_pool(key, part):
    full_shape = (POOL, PAGE, LAT + ROPE)
    sample = jnp.clip(jax.random.normal(jax.random.fold_in(key, 14), full_shape, jnp.float32), -6.0, 6.0)
    return sample.astype(jnp.bfloat16)


def draw_page_table(key, part):
    leaf_keys = jax.random.split(jax.random.fold_in(key, 21), LEAVES)

    def shuffle(leaf_key):
        return jax.random.permutation(leaf_key, POOL)
    orders = jax.vmap(shuffle)(leaf_keys)
    return orders[:, :MAXP].astype(jnp.int32)


def draw_context_lengths(key, part):
    drawn_len = jax.random.randint(jax.random.fold_in(key, 22), (LEAVES,), (MAXP - 1) * PAGE + 1, MAXP * PAGE + 1)
    return jnp.where(jnp.arange(LEAVES) == 0, MAXP * PAGE, drawn_len).astype(jnp.int32)


def draw_tree_parents(key, part):
    positions = jnp.arange(LOOK)
    upper_bound = jnp.maximum(positions, 1)
    parents_drawn = jax.random.randint(jax.random.fold_in(key, 23), (LEAVES, LOOK), 0, upper_bound[None, :])
    return jnp.where(positions[None, :] == 0, -1, parents_drawn).astype(jnp.int32)


def block_levels(own_key, shape, cuts, smallest, largest):
    level = 1.0
    for axis_at, shards_of in cuts:
        steps = jax.random.uniform(jax.random.fold_in(jax.random.fold_in(own_key, 6), axis_at), (shards_of,), jnp.float32, smallest / len(cuts), largest / len(cuts))
        level = level * jnp.repeat(jnp.exp(steps), shape[axis_at] // shards_of).reshape((-1,) + (1,) * (len(shape) - 1 - axis_at))
    return level


def routed_block(own_key, own, number, rows, number_of, top, most, slope):
    sequence = jax.random.permutation(own_key, number_of)
    packed, common = shares(number_of, rows * top, most, slope, True), shares(number_of, rows * top, most, slope, False)
    places = jnp.arange(number_of)

    def named(tallies, offset_by):
        used = int((tallies > 0).sum())
        fixed = max(1, used // 4)
        passed = fixed + (places - fixed + offset_by * (used - fixed)) % max(1, number_of - fixed)
        return jnp.zeros((number_of,), jnp.int32).at[sequence[jnp.where(places < fixed, places, passed)]].set(jnp.asarray(tallies, jnp.int32))

    tallies = jnp.where(number % 4 == 0, named(packed, number // 4), named(common, number - number // 4 - 1))
    mixed = jax.random.permutation(jax.random.fold_in(own, 3), number_of)
    source_of, taker = mixed[0:number_of // 2 * 2:2], mixed[1:number_of // 2 * 2:2]
    slack = jnp.minimum(tallies[source_of] - 1, most - tallies[taker]) // 2
    slack = jnp.where((source_of == sequence[0]) | (taker == sequence[0]) | (tallies[taker] == 0), 0, jnp.maximum(slack, 0))
    passed = jax.random.randint(jax.random.fold_in(own, 4), (number_of // 2,), 0, 1 << 20) % (slack + 1)
    tallies = tallies.at[source_of].add(-passed).at[taker].add(passed)
    items = jnp.searchsorted(jnp.cumsum(tallies), jnp.arange(rows * top), side="right").astype(jnp.int32)
    table = items.reshape(top, rows).T
    table = table[jax.random.permutation(jax.random.fold_in(own, 1), rows)]
    offset_by = jax.random.randint(jax.random.fold_in(own, 2), (rows, 1), 0, top)
    return jnp.take_along_axis(table, (jnp.arange(top)[None, :] + offset_by) % top, axis=1)


def shares(number_of, total, bound, lean, full):
    weights = [(1 << 20) // math.isqrt(rank ** lean) + 1 for rank in range(1, number_of + 1)]
    largest = bound if full else min(bound, max(-(-total // number_of), total * weights[0] // sum(weights)))
    least = 1 if total - largest >= number_of - 1 else 0
    holding, spare = [largest] + [least] * (number_of - 1), total - largest - least * (number_of - 1)
    while spare > 0:
        candidates = [i for i in range(1, number_of) if holding[i] < largest] or [i for i in range(1, number_of) if holding[i] < bound]
        whole, budget = sum([weights[i] for i in candidates]), spare
        for i in candidates:
            extra = min(bound - holding[i], max(1, budget * weights[i] // whole), spare)
            holding[i] = holding[i] + extra
            spare = spare - extra
    return np.array(holding)


def noise(rng, dims, deviation, reach, cuts=(), held_as=jnp.bfloat16):
    gain = block_levels(rng, dims, cuts, -0.22, 0.18) if cuts else 1.0
    result = jax.random.normal(rng, dims, jnp.float32) * deviation * gain
    return jnp.minimum(jnp.maximum(result, -reach), reach).astype(held_as)


def setup_inputs(seed: int = 0) -> dict:
    keys = jax.random.split(jax.random.key(seed), 17)
    queries = draw_queries(jax.random.fold_in(keys[16], 71), 0)
    key_lift = noise(keys[1], (HEADS, QK, LAT), QK ** -0.5, 0.5, ((0, 8),))
    value_lift = noise(keys[2], (HEADS, LAT, VD), LAT ** -0.5, 0.25, ((0, 8),))
    page_pool = draw_page_pool(jax.random.fold_in(keys[16], 71), 0)
    fresh_latents = noise(keys[4], (LEAVES, LOOK, CKV), 1.5, 6.0, ((0, 4),))
    page_table = draw_page_table(jax.random.fold_in(keys[16], 71), 0)
    context_lengths = draw_context_lengths(jax.random.fold_in(keys[16], 71), 0)
    tree_parents = draw_tree_parents(jax.random.fold_in(keys[16], 71), 0)
    out_weight = noise(keys[8], (HEADS * VD, D), VD ** -0.5, 0.5, ((0, 8), (1, 4)))
    residual = noise(keys[9], (ROWS, D), 1.0, 6.0, ((0, 8), (1, 4)))
    norm_gain = jnp.clip(jnp.exp(jax.random.uniform(keys[10], (D,), jnp.float32, math.log(0.5), math.log(2.0))), 0.5, 2.0)
    expert_ids_keys = jax.random.split(jax.random.fold_in(keys[11], 1), ROWS // ROW_DEV)
    expert_ids_turns = jax.random.permutation(jax.random.fold_in(keys[11], 3), ROWS // ROW_DEV)
    expert_ids = jax.vmap(lambda own, number: routed_block(jax.random.fold_in(keys[11], 2), own, number, ROW_DEV, EXPERTS, TOPK, CAP, 2))(expert_ids_keys, expert_ids_turns).reshape((ROWS, TOPK))
    route_weights = jnp.clip(0.1 + 0.5 * jax.random.uniform(keys[12], (ROWS, TOPK), jnp.float32) ** block_levels(keys[12], (ROWS, TOPK), ((0, 8),), -0.2, 0.2), 0.1, 0.6)
    gate_matrix = noise(keys[13], (EXPERTS, D, FFE), D ** -0.5, 0.0625, ((0, 8), (2, 4)))
    up_matrix = noise(keys[14], (EXPERTS, D, FFE), D ** -0.5, 0.0625, ((0, 8), (2, 4)))
    down_matrix = noise(keys[15], (EXPERTS, FFE, D), FFE ** -0.5, 0.1875, ((0, 8), (1, 4)))
    return dict(queries=queries, key_lift=key_lift, value_lift=value_lift, page_pool=page_pool, fresh_latents=fresh_latents, page_table=page_table, context_lengths=context_lengths, tree_parents=tree_parents, out_weight=out_weight, residual=residual, norm_gain=norm_gain, expert_ids=expert_ids, route_weights=route_weights, gate_matrix=gate_matrix, up_matrix=up_matrix, down_matrix=down_matrix)


NEGATIVE_FILL = -1e+30
NORM_EPSILON = 1e-06

def ancestry(tree_parents):
    advance = tree_parents.shape[1]
    positions = jnp.arange(advance, dtype=jnp.int32)
    current = jnp.broadcast_to(positions[None, :], tree_parents.shape).astype(jnp.int32)
    linked = current[:, :, None] == positions[None, None, :]
    for repeat in range(advance - 1):
        climbed = jnp.take_along_axis(tree_parents, jnp.maximum(current, 0), axis=1)
        current = jnp.where(current >= 0, climbed, -1).astype(jnp.int32)
        linked = linked | (current[:, :, None] == positions[None, None, :])
    return linked

def page_limits(page_table, context_lengths, first_page, page_count, page_len):
    page_ids = first_page + jnp.arange(page_count, dtype=jnp.int32)
    matches = page_table[:, :, None] == page_ids[None, None, :]
    offsets = jnp.arange(page_table.shape[1], dtype=jnp.int32) * page_len
    remain = context_lengths[:, None] - offsets[None, :]
    return lax.optimization_barrier(jnp.sum(jnp.where(matches, remain[:, :, None], 0), axis=1)).astype(jnp.int32)

def context_mask(limits, page_len, advance):
    within = jnp.arange(page_len, dtype=jnp.int32)
    visible = within[None, None, :] < limits[:, :, None]
    visible = visible.reshape(limits.shape[0], -1)
    return jnp.repeat(visible, advance, axis=0)

def normalize(values, norm_gain):
    floats = values.astype(jnp.float32)
    inverse = lax.rsqrt(lax.optimization_barrier(jnp.mean(floats * floats, axis=-1, keepdims=True)) + NORM_EPSILON)
    return (floats * inverse * norm_gain).astype(jnp.bfloat16)

def reference(queries, key_lift, value_lift, page_pool, fresh_latents, page_table, context_lengths, tree_parents, out_weight, residual, norm_gain, expert_ids, route_weights, gate_matrix, up_matrix, down_matrix):
    score_scale = (QK + ROPE) ** (-0.5)
    shaped = queries.reshape(ROWS, HEADS, QK + ROPE)
    limits = page_limits(page_table, context_lengths, 0, POOL, PAGE)
    row_mask = context_mask(limits, PAGE, LOOK)
    fresh_mask = ancestry(tree_parents)
    flat_keys = page_pool.reshape(POOL * PAGE, LAT + ROPE)
    fresh_float = fresh_latents.astype(jnp.float32)

    def one_head(head_items):
        head_query, lift_keys, lift_values = head_items
        latent = jnp.dot(head_query[:, :QK], lift_keys, preferred_element_type=jnp.float32).astype(jnp.bfloat16)
        joined_query = jnp.concatenate([latent, head_query[:, QK:]], axis=1)
        page_scores = jnp.dot(joined_query, flat_keys.T, preferred_element_type=jnp.float32) * score_scale
        page_scores = jnp.where(row_mask, page_scores, NEGATIVE_FILL)
        grouped = joined_query.reshape(LEAVES, LOOK, LAT + ROPE).astype(jnp.float32)
        fresh_scores = jnp.einsum('ltc,lsc->lts', grouped, fresh_float, precision=lax.Precision.HIGHEST) * score_scale
        fresh_scores = jnp.where(fresh_mask, fresh_scores, NEGATIVE_FILL)
        row_max = jnp.maximum(lax.optimization_barrier(jnp.max(page_scores, axis=1)), lax.optimization_barrier(jnp.max(fresh_scores, axis=2)).reshape(ROWS))
        page_exp = jnp.exp(page_scores - row_max[:, None])
        fresh_exp = jnp.exp(fresh_scores - row_max.reshape(LEAVES, LOOK)[:, :, None])
        totals = lax.optimization_barrier(jnp.sum(page_exp, axis=1)) + lax.optimization_barrier(jnp.sum(fresh_exp, axis=2)).reshape(ROWS)
        numerators = jnp.dot(page_exp.astype(jnp.bfloat16), flat_keys[:, :LAT], preferred_element_type=jnp.float32)
        fresh_numer = jnp.einsum('lts,lsc->ltc', fresh_exp.astype(jnp.bfloat16).astype(jnp.float32), fresh_float[:, :, :LAT], precision=lax.Precision.HIGHEST)
        numerators = numerators + fresh_numer.reshape(ROWS, LAT)
        projected = jnp.dot(numerators, lift_values.astype(jnp.float32), precision=lax.Precision.HIGHEST)
        return (projected / totals[:, None]).astype(jnp.bfloat16)
    attention = lax.map(one_head, (jnp.transpose(shaped, (1, 0, 2)), key_lift, value_lift))
    attention = jnp.transpose(attention, (1, 0, 2)).reshape(ROWS, HEADS * VD)
    head_output = jnp.dot(attention, out_weight, preferred_element_type=jnp.float32)
    hidden_state = (residual.astype(jnp.float32) + head_output).astype(jnp.bfloat16)
    normed = normalize(hidden_state, norm_gain)
    blocks = ROWS // ROW_DEV
    grouped_ids = expert_ids.reshape(blocks, ROW_DEV * TOPK)
    onehot = (grouped_ids[:, :, None] == jnp.arange(EXPERTS, dtype=jnp.int32)[None, None, :]).astype(jnp.int32)
    earlier = jnp.cumsum(onehot, axis=1) - onehot
    slot_index = lax.optimization_barrier(jnp.sum(earlier * onehot, axis=2)).astype(jnp.int32)
    column = (jnp.arange(blocks, dtype=jnp.int32)[:, None] * CAP + slot_index).reshape(-1).astype(jnp.int32)
    owners = (jnp.arange(ROWS * TOPK, dtype=jnp.int32) // TOPK).astype(jnp.int32)
    flat_ids = expert_ids.reshape(-1).astype(jnp.int32)
    slot_table = jnp.full((EXPERTS, blocks * CAP), ROWS, dtype=jnp.int32).at[flat_ids, column].set(owners)
    padded = jnp.concatenate([normed, jnp.zeros((1, D), jnp.bfloat16)], axis=0)

    def one_expert(expert_items):
        rows_index, gate_cols, up_cols, down_rows = expert_items
        inputs = padded[rows_index]
        gate_part = jnp.dot(inputs, gate_cols, preferred_element_type=jnp.float32)
        up_part = jnp.dot(inputs, up_cols, preferred_element_type=jnp.float32)
        active = (jax.nn.silu(gate_part) * up_part).astype(jnp.bfloat16)
        return jnp.dot(active, down_rows, preferred_element_type=jnp.float32).astype(jnp.bfloat16)
    results = lax.map(one_expert, (slot_table, gate_matrix, up_matrix, down_matrix))
    picked = results[flat_ids, column].reshape(ROWS, TOPK, D).astype(jnp.float32)
    mixed_sum = lax.optimization_barrier(jnp.sum(route_weights[:, :, None] * picked, axis=1))
    return (hidden_state.astype(jnp.float32) + mixed_sum).astype(jnp.bfloat16)
```

```python
import functools

import jax
import jax.numpy as jnp
from jax import lax
from jax.experimental import pallas as pl
from jax.experimental.pallas import tpu as pltpu
from jax.sharding import PartitionSpec as P

LAT = 512
ROPE = 64
QK = 128
VD = 128
NEG = -(2.0**100)
EPS = 1e-06
F32 = jnp.float32
BF16 = jnp.bfloat16
MESH = pl.DeviceIdType.MESH
STAT = 128


def iota(shape, dim):
    return lax.broadcasted_iota(jnp.int32, shape, dim)


def dot(a, b):
    return jnp.dot(a, b, preferred_element_type=F32)


def dot_t(a, b):
    return lax.dot_general(a, b, (((1,), (1,)), ((), ())), preferred_element_type=F32)


def spread(per_leaf, advance):
    leaves, n = per_leaf.shape
    return jnp.broadcast_to(per_leaf[:, None, :], (leaves, advance, n)).reshape(leaves * advance, n)


def masks(c, pt_ref, cl_ref, tp_ref, pool_keys, page_len, fresh_cols, own_leaves):
    leaves, slots = pt_ref.shape
    advance = tp_ref.shape[1]
    rows = leaves * advance
    lengths = jnp.sum(
        jnp.where(
            iota((leaves, leaves), 0) == iota((leaves, leaves), 1),
            jnp.broadcast_to(cl_ref[...].astype(F32), (leaves, leaves)),
            0.0,
        ),
        axis=1,
        keepdims=True,
    )
    remain = lengths - (iota((leaves, slots), 1) * page_len).astype(F32)
    table = pt_ref[...]
    lane = iota((leaves, pool_keys), 1)
    limit = jnp.zeros((leaves, pool_keys), F32)
    pages = pool_keys // page_len
    for p in range(pages):
        here = jnp.sum(jnp.where(table == c * pages + p, remain, 0.0), axis=1, keepdims=True)
        limit = jnp.where(lane // page_len == p, here, limit)
    limit = spread(limit, advance)
    pool_mask = (iota((rows, pool_keys), 1) % page_len).astype(F32) < limit
    token = iota((leaves, fresh_cols), 1) % advance
    parents = tp_ref[...]
    chains = [jnp.where(token == 0, 1.0, 0.0)]
    for t in range(1, advance):
        chain = jnp.where(token == t, 1.0, 0.0)
        for u in range(t):
            chain = jnp.where(parents[:, t : t + 1] == u, chain + chains[u], chain)
        chains.append(chain)
    row = iota((rows, fresh_cols), 0)
    col = iota((rows, fresh_cols), 1)
    linked = jnp.zeros((rows, fresh_cols), F32)
    for t in range(advance):
        linked = jnp.where(row % advance == t, spread(chains[t], advance), linked)
    own = (row // advance == c * own_leaves + col // advance) & (col < own_leaves * advance)
    fresh_mask = (linked > 0.5) & own
    return pool_mask, fresh_mask


def kernel(
    nctx, nexp, page_len, own_leaves,
    q_ref, kl_ref, vl_ref, pool_ref, fresh_ref, pt_ref, cl_ref, tp_ref, ow_hbm, res_ref, gain_ref, ids_ref,
    rw_ref, g_hbm, u_hbm, d_hbm, out_ref,
    kf, att_send, att_recv, w2, g_v, u_v, d_v, w_all, zf, zs, zr, xg, pf, ps, pr, cs, cr, yf, ys, yr,
    loc, att_ss, att_rs, w2_ss, w2_rs, w_ss, w_rs, wp_ss, wp_rs, z_ss, z_rs, agz_ss, agz_rs, agc_ss, agc_rs,
    agp_ss, agp_rs, p_ss, p_rs, c_ss, c_rs, y_ss, y_rs,
):
    c = lax.axis_index("context")
    e = lax.axis_index("expert")
    k, z = e % 2, e // 2
    nz = nexp // 2
    rows = q_ref.shape[0]
    half_rows = rows // 2
    heads = kl_ref.shape[0]
    row_dev, cols = res_ref.shape
    half = cols // 2
    other = 1 - k

    def ctx(d):
        return ((c // 2 + d // 2) % (nctx // 2)) * 2 + (c + d) % 2

    def dev(cc, zz, kk):
        return (cc, zz * 2 + kk)

    def send(src, dst, ss, rs, to):
        return pltpu.make_async_remote_copy(
            src_ref=src, dst_ref=dst, send_sem=ss, recv_sem=rs, device_id=to, device_id_type=MESH
        )

    def got(dst, ss, rs):
        send(dst, dst, ss, rs, dev(c, z, other)).wait_recv()

    def z_loop(body):
        lax.fori_loop(1, nz, lambda d, carry: (body((z + d) % nz), carry)[1], 0)

    barrier = pltpu.get_barrier_semaphore()
    for d in range(nctx):
        for kk in range(2):
            if d or kk:
                pl.semaphore_signal(
                    barrier, inc=1, device_id=dev(ctx(d), z, (k + kk) % 2), device_id_type=MESH
                )
    z_loop(lambda zp: pl.semaphore_signal(barrier, inc=1, device_id=dev(c, zp, k), device_id_type=MESH))

    local = [
        pltpu.make_async_copy(ow_hbm, w2.at[k], loc.at[0]),
        pltpu.make_async_copy(g_hbm, g_v, loc.at[1]),
        pltpu.make_async_copy(u_hbm, u_v, loc.at[2]),
        pltpu.make_async_copy(d_hbm, d_v, loc.at[3]),
    ]
    for copy in local:
        copy.start()

    lane_w = iota((row_dev, STAT), 1)
    dense = jnp.zeros((row_dev, STAT), F32)
    ids, rw = ids_ref[...], rw_ref[...]
    for t in range(ids.shape[1]):
        dense = jnp.where(lane_w == ids[:, t : t + 1], rw[:, t : t + 1], dense)
    w_all[k, z] = dense

    pool_keys = pool_ref.shape[0]
    fresh_keys = fresh_ref.shape[0]
    fresh_cols = kf.shape[0]
    if fresh_cols != fresh_keys:
        kf[...] = jnp.zeros(kf.shape, BF16)
    kf[0:fresh_keys, :] = fresh_ref[...]
    pool_mask, fresh_mask = masks(
        c, pt_ref, cl_ref, tp_ref, pool_keys, page_len, fresh_cols, own_leaves
    )
    qf = q_ref[...].astype(F32)
    scale = (QK + ROPE) ** (-0.5)
    kp = pool_ref[...]
    kfv = kf[...]
    parts = []
    lane_s = iota((rows, STAT), 1)
    stats = jnp.zeros((rows, STAT), F32)
    for h in range(heads):
        at = h * (QK + ROPE)
        lat = dot(qf[:, at : at + QK].astype(BF16), kl_ref[h]).astype(BF16)
        rot = qf[:, at + QK : at + QK + ROPE].astype(BF16)
        sp = (dot_t(lat, kp[:, :LAT]) + dot_t(rot, kp[:, LAT:])) * scale
        sf = (dot_t(lat, kfv[:, :LAT]) + dot_t(rot, kfv[:, LAT:])) * scale
        sp = jnp.where(pool_mask, sp, NEG)
        sf = jnp.where(fresh_mask, sf, NEG)
        top = jnp.maximum(
            jnp.max(sp, axis=1, keepdims=True), jnp.max(sf, axis=1, keepdims=True)
        )
        top = top.astype(BF16).astype(F32)
        ep, ef = jnp.exp(sp - top), jnp.exp(sf - top)
        total = jnp.sum(ep, axis=1, keepdims=True) + jnp.sum(ef, axis=1, keepdims=True)
        numer = dot(ep.astype(BF16), kp[:, :LAT]) + dot(ef.astype(BF16), kfv[:, :LAT])
        numer = numer / total
        high = numer.astype(BF16)
        low = (numer - high.astype(F32)).astype(BF16)
        parts.append(dot(high, vl_ref[h]) + dot(low, vl_ref[h]))
        t_high = total.astype(BF16).astype(F32)
        for i, value in enumerate((top, t_high, total - t_high)):
            stats = jnp.where(lane_s == 3 * h + i, value, stats)
    width = heads * VD + STAT
    message = jnp.concatenate(parts + [stats], axis=1).reshape(nz, 2, row_dev, width)
    for kk in range(2):
        att_send[kk] = message[:, kk].reshape(half_rows, width).astype(BF16)
    att_recv[c * 2 + k] = att_send[k]

    pl.semaphore_wait(barrier, 2 * nctx - 1 + nz - 1)
    att_copies = []
    for d in range(nctx - 1, -1, -1):
        for kk in range(2):
            if d or kk:
                to = (k + kk) % 2
                att_copies.append(
                    send(att_send.at[to], att_recv.at[c * 2 + k], att_ss.at[2 * d + kk], att_rs.at[c * 2 + k],
                         dev(ctx(d), z, to))
                )
                att_copies[-1].start()
    w2_copy = send(ow_hbm, w2.at[k], w2_ss, w2_rs, dev(c, z, other))
    w2_copy.start()
    z_loop(lambda zp: send(w_all.at[k, z], w_all.at[k, z], w_ss.at[zp], w_rs.at[z], dev(c, zp, k)).start())
    for d in range(nctx):
        for kk in range(2):
            if d or kk:
                slot = ctx(d) * 2 + (k + kk) % 2
                got(att_recv.at[slot], att_ss.at[0], att_rs.at[slot])

    merged = []
    for kk in range(2):
        held = [att_recv[cc * 2 + kk].astype(F32) for cc in range(nctx)]
        for h in range(heads):
            base = heads * VD + 3 * h
            tops = [v[:, base : base + 1] for v in held]
            best = functools.reduce(jnp.maximum, tops)
            shares = [
                (v[:, base + 1 : base + 2] + v[:, base + 2 : base + 3]) * jnp.exp(t - best)
                for v, t in zip(held, tops)
            ]
            whole = functools.reduce(jnp.add, shares)
            mixed = functools.reduce(
                jnp.add, [s * v[:, h * VD : (h + 1) * VD] for s, v in zip(shares, held)]
            )
            merged.append((mixed / whole).astype(BF16))
    local[0].wait()
    got(w2.at[other], w2_ss, w2_rs)
    span = heads
    projected = dot(jnp.concatenate(merged[:span], axis=1), w2[0]) + dot(
        jnp.concatenate(merged[span:], axis=1), w2[1]
    )

    def fold(v):
        v = v.reshape(-1, row_dev, cols)
        return jnp.concatenate([v[:, :, :half], v[:, :, half:]], axis=1)

    folded = fold(projected)
    zf[...] = folded
    zs[...] = folded.astype(BF16)
    z_loop(lambda zp: send(zs.at[zp], zr.at[z], z_ss.at[zp], z_rs.at[z], dev(c, zp, k)).start())
    state = zf[z] + fold(res_ref[...].astype(F32))[0]

    def take(d, acc):
        zp = (z + d) % nz
        got(zr.at[zp], z_ss.at[zp], z_rs.at[zp])
        return acc + zr[zp].astype(F32)

    state = lax.fori_loop(1, nz, take, state)
    hidden = state.astype(BF16)
    xg[c, k, z] = hidden

    def ag_z(zp):
        return send(xg.at[c, k, z], xg.at[c, k, z], agz_ss.at[zp], agz_rs.at[z], dev(c, zp, k))

    def ag_c(d, zp):
        piece = xg.at[c, k, zp]
        return send(piece, piece, agc_ss.at[d, zp], agc_rs.at[c, zp], dev(ctx(d), z, k))

    def ag_p(cc, zp):
        piece = xg.at[cc, k, zp]
        return send(piece, piece, agp_ss.at[cc, zp], agp_rs.at[cc, zp], dev(c, z, other))

    z_loop(lambda zp: ag_z(zp).start())

    def onward(zp):
        for d in range(1, nctx - 1):
            ag_c(d, zp).start()
        ag_p(c, zp).start()

    onward(z)

    def arrived(zp):
        got(xg.at[c, k, zp], agz_ss.at[zp], agz_rs.at[zp])
        onward(zp)

    z_loop(arrived)
    lax.fori_loop(0, nz, lambda zp, carry: (ag_c(nctx - 1, zp).start(), carry)[1], 0)

    z_loop(lambda zp: got(w_all.at[k, zp], w_ss.at[zp], w_rs.at[zp]))
    wp_copy = send(w_all.at[k], w_all.at[k], wp_ss, wp_rs, dev(c, z, other))
    wp_copy.start()

    def relay(d):
        cc = ctx(d)

        def body(zp, carry):
            got(xg.at[cc, k, zp], agc_ss.at[0, zp], agc_rs.at[cc, zp])
            ag_p(cc, zp).start()
            return carry

        lax.fori_loop(0, nz, body, 0)

    local[1].wait()
    local[2].wait()
    acc = [jnp.zeros((rows, 1), F32), jnp.zeros((rows, g_v.shape[1]), F32), jnp.zeros((rows, g_v.shape[1]), F32)]

    def expand(d):
        cc = ctx(d)

        def body(zp, carry):
            got(xg.at[cc, other, zp], agp_ss.at[cc, zp], agp_rs.at[cc, zp])
            return carry

        lax.fori_loop(0, nz, body, 0)
        both = [xg[cc, kk].astype(F32) for kk in (k, other)]
        for i in range(2):
            x = jnp.concatenate(
                [v[:, i * row_dev : (i + 1) * row_dev].reshape(half_rows, half) for v in both], axis=0
            )
            at = pl.ds(pl.multiple_of(cc * cols + i * half, half), half)
            scaled = (x * gain_ref[:, at]).astype(BF16)
            acc[0] = acc[0] + jnp.sum(x * x, axis=1, keepdims=True)
            acc[1] = acc[1] + dot(scaled, g_v[at, :])
            acc[2] = acc[2] + dot(scaled, u_v[at, :])

    relay(1)
    expand(0)
    for d in range(2, nctx):
        relay(d)
        expand(d - 1)
    expand(nctx - 1)

    inverse = lax.rsqrt(acc[0] * (1.0 / (nctx * cols)) + EPS)
    gate, up = acc[1] * inverse, acc[2] * inverse
    got(w_all.at[other], wp_ss, wp_rs)
    weights = jnp.concatenate(
        [w_all[kk].reshape(half_rows, STAT) for kk in (k, other)], axis=0
    )
    weight = jnp.sum(jnp.where(iota((rows, STAT), 1) == e, weights, 0.0), axis=1, keepdims=True)
    active = jnp.where(weight > 0.0, gate / (1.0 + jnp.exp(-gate)) * up, 0.0).astype(BF16)
    local[3].wait()

    def contract(d):
        at = pl.ds(pl.multiple_of(ctx(d) * cols, cols), cols)
        out = dot(active, d_v[:, at]) * weight
        pf[d] = out[:half_rows]
        ps[d] = out[half_rows:].astype(BF16)
        pair(d).start()

    def pair(d):
        return send(ps.at[d], pr.at[d], p_ss.at[d], p_rs.at[d], dev(c, z, other))

    def across(d):
        return send(cs.at[d], cr.at[c], c_ss.at[d], c_rs.at[c], dev(ctx(d), z, k))

    def join(d):
        got(pr.at[d], p_ss.at[d], p_rs.at[d])
        both = pf[d] + pr[d].astype(F32)
        if d:
            cs[d] = both.astype(BF16)
            across(d).start()
        return both

    order = list(range(nctx - 1, -1, -1))
    contract(order[0])
    for before, now in zip(order[:-1], order[1:]):
        contract(now)
        join(before)
    total = join(0)
    for d in range(1, nctx):
        cc = ctx(d)
        got(cr.at[cc], c_ss.at[d], c_rs.at[cc])
        total = total + cr[cc].astype(F32)

    folded = fold(total)
    yf[...] = folded
    ys[...] = folded.astype(BF16)
    z_loop(lambda zp: send(ys.at[zp], yr.at[z], y_ss.at[zp], y_rs.at[z], dev(c, zp, k)).start())
    result = hidden.astype(F32) + yf[z]

    def take_last(d, acc):
        zp = (z + d) % nz
        got(yr.at[zp], y_ss.at[zp], y_rs.at[zp])
        return acc + yr[zp].astype(F32)

    result = lax.fori_loop(1, nz, take_last, result)
    out_ref[...] = jnp.concatenate([result[:row_dev], result[row_dev:]], axis=1).astype(BF16)

    for copy in att_copies:
        copy.wait_send()
    w2_copy.wait_send()
    wp_copy.wait_send()

    def drain_z(zp):
        send(w_all.at[k, z], w_all.at[k, z], w_ss.at[zp], w_rs.at[z], dev(c, zp, k)).wait_send()
        send(zs.at[zp], zr.at[z], z_ss.at[zp], z_rs.at[z], dev(c, zp, k)).wait_send()
        ag_z(zp).wait_send()
        send(ys.at[zp], yr.at[z], y_ss.at[zp], y_rs.at[z], dev(c, zp, k)).wait_send()

    z_loop(drain_z)

    def drain(zp, carry):
        for d in range(nctx):
            if d:
                ag_c(d, zp).wait_send()
            ag_p(ctx(d), zp).wait_send()
        return carry

    lax.fori_loop(0, nz, drain, 0)
    for d in range(nctx):
        pair(d).wait_send()
        if d:
            across(d).wait_send()


def local(
    nctx, nexp,
    queries, key_lift, value_lift, page_pool, fresh_latents, page_table, context_lengths, tree_parents,
    out_weight, residual, norm_gain, expert_ids, route_weights, gate_matrix, up_matrix, down_matrix,
):
    nz = nexp // 2
    rows = queries.shape[0]
    half_rows = rows // 2
    row_dev, cols = residual.shape
    half = cols // 2
    heads = key_lift.shape[0]
    width = heads * VD + STAT
    own_leaves, advance, ckv = fresh_latents.shape
    fresh_cols = -(-own_leaves * advance // 128) * 128
    gate, up, down = gate_matrix[0], up_matrix[0], down_matrix[0]
    dma = pltpu.SemaphoreType.DMA
    vm = pl.BlockSpec(memory_space=pltpu.VMEM)
    hbm = pl.BlockSpec(memory_space=pl.ANY)
    piece = (2 * row_dev, half)
    scratch = [
        pltpu.VMEM((fresh_cols, ckv), BF16),
        pltpu.VMEM((2, half_rows, width), BF16),
        pltpu.VMEM((2 * nctx, half_rows, width), BF16),
        pltpu.VMEM((2,) + out_weight.shape, BF16),
        pltpu.VMEM(gate.shape, BF16),
        pltpu.VMEM(up.shape, BF16),
        pltpu.VMEM(down.shape, BF16),
        pltpu.VMEM((2, nz, row_dev, STAT), F32),
        pltpu.VMEM((nz,) + piece, F32),
        pltpu.VMEM((nz,) + piece, BF16),
        pltpu.VMEM((nz,) + piece, BF16),
        pltpu.VMEM((nctx, 2, nz) + piece, BF16),
        pltpu.VMEM((nctx, half_rows, cols), F32),
        pltpu.VMEM((nctx, half_rows, cols), BF16),
        pltpu.VMEM((nctx, half_rows, cols), BF16),
        pltpu.VMEM((nctx, half_rows, cols), BF16),
        pltpu.VMEM((nctx, half_rows, cols), BF16),
        pltpu.VMEM((nz,) + piece, F32),
        pltpu.VMEM((nz,) + piece, BF16),
        pltpu.VMEM((nz,) + piece, BF16),
        dma((4,)),
        dma((2 * nctx,)), dma((2 * nctx,)),
        dma, dma,
        dma((nz,)), dma((nz,)),
        dma, dma,
        dma((nz,)), dma((nz,)),
        dma((nz,)), dma((nz,)),
        dma((nctx, nz)), dma((nctx, nz)),
        dma((nctx, nz)), dma((nctx, nz)),
        dma((nctx,)), dma((nctx,)),
        dma((nctx,)), dma((nctx,)),
        dma((nz,)), dma((nz,)),
    ]
    return pl.pallas_call(
        functools.partial(kernel, nctx, nexp, page_pool.shape[1], own_leaves),
        out_shape=jax.ShapeDtypeStruct((row_dev, cols), BF16),
        in_specs=[vm] * 8 + [hbm] + [vm] * 4 + [hbm] * 3,
        out_specs=vm,
        scratch_shapes=scratch,
        compiler_params=pltpu.CompilerParams(
            collective_id=0, has_side_effects=True, vmem_limit_bytes=60 * 2**20
        ),
    )(
        queries, key_lift, value_lift, page_pool.reshape(-1, ckv), fresh_latents.reshape(-1, ckv), page_table,
        context_lengths.reshape(1, -1), tree_parents, out_weight, residual, norm_gain.reshape(1, -1),
        expert_ids, route_weights, gate, up, down,
    )


def solution(mesh):
    return jax.shard_map(
        functools.partial(local, mesh.shape["context"], mesh.shape["expert"]),
        mesh=mesh,
        in_specs=(
            P(None, "expert"),
            P("expert", None, None),
            P("expert", None, None),
            P("context", None, None),
            P("context", None, None),
            P(),
            P(),
            P(),
            P("expert", "context"),
            P("expert", "context"),
            P(),
            P("expert", None),
            P("expert", None),
            P("expert", None, "context"),
            P("expert", None, "context"),
            P("expert", "context", None),
        ),
        out_specs=P("expert", "context"),
        check_vma=False,
    )
```

```python
import functools

import jax
import jax.numpy as jnp
from jax import lax
from jax.experimental import pallas as pl
from jax.experimental.pallas import tpu as pltpu
from jax.sharding import PartitionSpec as P

LAT = 512
ROPE = 64
QK = 128
VD = 128
NEG = -(2.0**100)
EPS = 1e-06
F32 = jnp.float32
BF16 = jnp.bfloat16
MESH = pl.DeviceIdType.MESH
STAT = 128


def iota(shape, dim):
    return lax.broadcasted_iota(jnp.int32, shape, dim)


def dot(a, b):
    return jnp.dot(a, b, preferred_element_type=F32)


def dot_t(a, b):
    return lax.dot_general(a, b, (((1,), (1,)), ((), ())), preferred_element_type=F32)


def div(v, n):
    return jnp.right_shift(v, n.bit_length() - 1) if n & (n - 1) == 0 else v // n


def mod(v, n):
    return v & (n - 1) if n & (n - 1) == 0 else v % n


def spread(per_leaf, advance):
    leaves, n = per_leaf.shape
    return jnp.broadcast_to(per_leaf[:, None, :], (leaves, advance, n)).reshape(leaves * advance, n)


def masks(c, pt_ref, cl_ref, tp_ref, pool_keys, page_len, fresh_cols, own_leaves):
    leaves, slots = pt_ref.shape
    advance = tp_ref.shape[1]
    rows = leaves * advance
    lengths = jnp.sum(
        jnp.where(
            iota((leaves, leaves), 0) == iota((leaves, leaves), 1),
            jnp.broadcast_to(cl_ref[...].astype(F32), (leaves, leaves)),
            0.0,
        ),
        axis=1,
        keepdims=True,
    )
    remain = lengths - (iota((leaves, slots), 1) * page_len).astype(F32)
    table = pt_ref[...]
    lane = iota((leaves, pool_keys), 1)
    limit = jnp.zeros((leaves, pool_keys), F32)
    pages = pool_keys // page_len
    for p in range(pages):
        here = jnp.sum(jnp.where(table == c * pages + p, remain, 0.0), axis=1, keepdims=True)
        limit = jnp.where(div(lane, page_len) == p, here, limit)
    inside = jnp.where(mod(lane, page_len).astype(F32) < limit, 1.0, 0.0)
    pool_mask = spread(inside, advance)
    token = mod(iota((leaves, fresh_cols), 1), advance)
    parents = tp_ref[...]
    chains = [jnp.where(token == 0, 1.0, 0.0)]
    for t in range(1, advance):
        chain = jnp.where(token == t, 1.0, 0.0)
        for u in range(t):
            chain = jnp.where(parents[:, t : t + 1] == u, chain + chains[u], chain)
        chains.append(chain)
    row = iota((rows, fresh_cols), 0)
    col = iota((rows, fresh_cols), 1)
    linked = jnp.zeros((rows, fresh_cols), F32)
    for t in range(advance):
        linked = jnp.where(mod(row, advance) == t, spread(chains[t], advance), linked)
    own = (div(row, advance) == c * own_leaves + div(col, advance)) & (col < own_leaves * advance)
    fresh_mask = jnp.where(own, linked, 0.0)
    return jnp.concatenate([pool_mask, fresh_mask], axis=1) > 0.5


def kernel(
    nctx, nexp, page_len, own_leaves,
    q_ref, kl_ref, vl_ref, pool_ref, fresh_ref, pt_ref, cl_ref, tp_ref, ow_hbm, res_ref, gain_ref, ids_ref,
    rw_ref, g_hbm, u_hbm, d_hbm, out_ref,
    kf, att_send, att_recv, w2, g_v, u_v, d_v, w_all, zf, zs, zr, xg, pf, ps, pr, cs, cr, yf, ys, yr,
    loc, att_ss, att_rs, w2_ss, w2_rs, w_ss, w_rs, wp_ss, wp_rs, z_ss, z_rs, agz_ss, agz_rs, agc_ss, agc_rs,
    agp_ss, agp_rs, p_ss, p_rs, c_ss, c_rs, y_ss, y_rs,
):
    c = lax.axis_index("context")
    e = lax.axis_index("expert")
    k, z = e % 2, e // 2
    nz = nexp // 2
    rows = q_ref.shape[0]
    half_rows = rows // 2
    heads = kl_ref.shape[0]
    row_dev, cols = res_ref.shape
    half = cols // 2
    other = 1 - k

    near = [((c // 2 + d // 2) % (nctx // 2)) * 2 + (c + d) % 2 for d in range(nctx)]
    turn = 1 - 2 * (z // (nz // 2))

    def ctx(d):
        return near[d]

    def zat(d):
        return (z + turn * d + nz) % nz

    def dev(cc, zz, kk):
        return (cc, zz * 2 + kk)

    def send(src, dst, ss, rs, to):
        return pltpu.make_async_remote_copy(
            src_ref=src, dst_ref=dst, send_sem=ss, recv_sem=rs, device_id=to, device_id_type=MESH
        )

    def got(dst, ss, rs):
        send(dst, dst, ss, rs, dev(c, z, other)).wait_recv()

    def z_loop(body):
        lax.fori_loop(1, nz, lambda d, carry: (body(zat(d)), carry)[1], 0)

    barrier = pltpu.get_barrier_semaphore()
    for d in range(nctx):
        for kk in range(2):
            if d or kk:
                pl.semaphore_signal(
                    barrier, inc=1, device_id=dev(ctx(d), z, (k + kk) % 2), device_id_type=MESH
                )
    z_loop(lambda zp: pl.semaphore_signal(barrier, inc=1, device_id=dev(c, zp, k), device_id_type=MESH))

    local = [
        pltpu.make_async_copy(ow_hbm, w2.at[k], loc.at[0]),
        pltpu.make_async_copy(g_hbm, g_v, loc.at[1]),
        pltpu.make_async_copy(u_hbm, u_v, loc.at[2]),
        pltpu.make_async_copy(d_hbm, d_v, loc.at[3]),
    ]
    for copy in local:
        copy.start()

    lane_w = iota((row_dev, STAT), 1)
    dense = jnp.zeros((row_dev, STAT), F32)
    ids, rw = ids_ref[...], rw_ref[...]
    for t in range(ids.shape[1]):
        dense = jnp.where(lane_w == ids[:, t : t + 1], rw[:, t : t + 1], dense)
    w_all[k, z] = dense

    pool_keys = pool_ref.shape[0]
    fresh_keys = fresh_ref.shape[0]
    fresh_cols = kf.shape[0] - pool_keys
    if fresh_cols != fresh_keys:
        kf[pool_keys:, :] = jnp.zeros((fresh_cols, kf.shape[1]), BF16)
    kf[0:pool_keys, :] = pool_ref[...]
    kf[pool_keys : pool_keys + fresh_keys, :] = fresh_ref[...]
    mask = masks(c, pt_ref, cl_ref, tp_ref, pool_keys, page_len, fresh_cols, own_leaves)
    qf = q_ref[...].astype(F32)
    scale = (QK + ROPE) ** (-0.5)
    keys = kf[...]
    lat, rot = [], []
    for h in range(heads):
        at = h * (QK + ROPE)
        lat.append(dot(qf[:, at : at + QK].astype(BF16), kl_ref[h]).astype(BF16))
        rot.append(qf[:, at + QK : at + QK + ROPE].astype(BF16))
    scores = dot_t(jnp.concatenate(lat, axis=0), keys[:, :LAT])
    scores = (scores + dot_t(jnp.concatenate(rot, axis=0), keys[:, LAT:])) * scale
    scores = jnp.concatenate(
        [jnp.where(mask, scores[h * rows : (h + 1) * rows], NEG) for h in range(heads)], axis=0
    )
    top = jnp.max(scores, axis=1, keepdims=True).astype(BF16).astype(F32)
    weight = jnp.exp(scores - top)
    total = jnp.sum(weight, axis=1, keepdims=True)
    numer = dot(weight.astype(BF16), keys[:, :LAT]) / total
    high = numer.astype(BF16)
    low = (numer - high.astype(F32)).astype(BF16)
    t_high = total.astype(BF16).astype(F32)
    parts = []
    lane_s = iota((rows, STAT), 1)
    stats = jnp.zeros((rows, STAT), F32)
    for h in range(heads):
        own = slice(h * rows, (h + 1) * rows)
        parts.append(dot(high[own], vl_ref[h]) + dot(low[own], vl_ref[h]))
        for i, value in enumerate((top, t_high, total - t_high)):
            stats = jnp.where(lane_s == 3 * h + i, value[own], stats)
    width = heads * VD + STAT
    message = jnp.concatenate(parts + [stats], axis=1).reshape(nz, 2, row_dev, width)
    for kk in range(2):
        att_send[kk] = message[:, kk].reshape(half_rows, width).astype(BF16)
    att_recv[c * 2 + k] = att_send[k]

    pl.semaphore_wait(barrier, 2 * nctx - 1 + nz - 1)
    att_copies = []
    for d in range(nctx - 1, -1, -1):
        for kk in range(2):
            if d or kk:
                to = (k + kk) % 2
                att_copies.append(
                    send(att_send.at[to], att_recv.at[c * 2 + k], att_ss.at[2 * d + kk], att_rs.at[c * 2 + k],
                         dev(ctx(d), z, to))
                )
                att_copies[-1].start()
    w2_copy = send(ow_hbm, w2.at[k], w2_ss, w2_rs, dev(c, z, other))
    w2_copy.start()
    z_loop(lambda zp: send(w_all.at[k, z], w_all.at[k, z], w_ss.at[zp], w_rs.at[z], dev(c, zp, k)).start())
    for d in range(nctx):
        for kk in range(2):
            if d or kk:
                slot = ctx(d) * 2 + (k + kk) % 2
                got(att_recv.at[slot], att_ss.at[0], att_rs.at[slot])

    merged = []
    for kk in range(2):
        held = [att_recv[cc * 2 + kk].astype(F32) for cc in range(nctx)]
        for h in range(heads):
            base = heads * VD + 3 * h
            tops = [v[:, base : base + 1] for v in held]
            best = functools.reduce(jnp.maximum, tops)
            shares = [
                (v[:, base + 1 : base + 2] + v[:, base + 2 : base + 3]) * jnp.exp(t - best)
                for v, t in zip(held, tops)
            ]
            whole = functools.reduce(jnp.add, shares)
            mixed = functools.reduce(
                jnp.add, [s * v[:, h * VD : (h + 1) * VD] for s, v in zip(shares, held)]
            )
            merged.append((mixed / whole).astype(BF16))
    local[0].wait()
    got(w2.at[other], w2_ss, w2_rs)
    span = heads
    projected = dot(jnp.concatenate(merged[:span], axis=1), w2[0]) + dot(
        jnp.concatenate(merged[span:], axis=1), w2[1]
    )

    def fold(v):
        v = v.reshape(-1, row_dev, cols)
        return jnp.concatenate([v[:, :, :half], v[:, :, half:]], axis=1)

    folded = fold(projected)
    zf[...] = folded
    zs[...] = folded.astype(BF16)
    z_loop(lambda zp: send(zs.at[zp], zr.at[z], z_ss.at[zp], z_rs.at[z], dev(c, zp, k)).start())
    state = zf[z] + fold(res_ref[...].astype(F32))[0]

    def take(d, acc):
        zp = zat(d)
        got(zr.at[zp], z_ss.at[zp], z_rs.at[zp])
        return acc + zr[zp].astype(F32)

    state = lax.fori_loop(1, nz, take, state)
    hidden = state.astype(BF16)
    xg[c, k, z] = hidden

    def ag_z(zp):
        return send(xg.at[c, k, z], xg.at[c, k, z], agz_ss.at[zp], agz_rs.at[z], dev(c, zp, k))

    def ag_c(d, zp):
        piece = xg.at[c, k, zp]
        return send(piece, piece, agc_ss.at[d, zp], agc_rs.at[c, zp], dev(ctx(d), z, k))

    def ag_p(cc, zp):
        piece = xg.at[cc, k, zp]
        return send(piece, piece, agp_ss.at[cc, zp], agp_rs.at[cc, zp], dev(c, z, other))

    z_loop(lambda zp: ag_z(zp).start())

    def onward(zp):
        for d in (1, 2):
            ag_c(d, zp).start()
        ag_p(c, zp).start()

    def ag_far(d, zp):
        piece = xg.at[ctx(d), k, zp]
        return send(piece, piece, agc_ss.at[3, zp], agc_rs.at[ctx(d), zp], dev(ctx(3 - d), z, k))

    def relay(d, zp, far):
        got(xg.at[ctx(d), k, zp], agc_ss.at[0, zp], agc_rs.at[ctx(d), zp])
        if far:
            ag_far(d, zp).start()
        ag_p(ctx(d), zp).start()

    def steps(low, up, far):
        def body(d, carry):
            zp, last = zat(d), zat(d - 1)
            got(xg.at[c, k, zp], agz_ss.at[zp], agz_rs.at[zp])
            onward(zp)
            for n in (1, 2):
                relay(n, last, n == far)
            return carry

        lax.fori_loop(low, up, body, 0)

    onward(z)
    steps(1, nz // 2 + 1, 1)
    steps(nz // 2 + 1, nz, 2)
    for n in (1, 2):
        relay(n, zat(nz - 1), n == 2)

    z_loop(lambda zp: got(w_all.at[k, zp], w_ss.at[zp], w_rs.at[zp]))
    wp_copy = send(w_all.at[k], w_all.at[k], wp_ss, wp_rs, dev(c, z, other))
    wp_copy.start()

    local[1].wait()
    local[2].wait()
    acc = [jnp.zeros((rows, 1), F32), jnp.zeros((rows, g_v.shape[1]), F32), jnp.zeros((rows, g_v.shape[1]), F32)]

    def expand(d):
        cc = ctx(d)

        def body(zp, carry):
            got(xg.at[cc, other, zp], agp_ss.at[cc, zp], agp_rs.at[cc, zp])
            return carry

        lax.fori_loop(0, nz, body, 0)
        both = [xg[cc, kk].astype(F32) for kk in (k, other)]
        for i in range(2):
            x = jnp.concatenate(
                [v[:, i * row_dev : (i + 1) * row_dev].reshape(half_rows, half) for v in both], axis=0
            )
            at = pl.ds(pl.multiple_of(cc * cols + i * half, half), half)
            scaled = (x * gain_ref[:, at]).astype(BF16)
            acc[0] = acc[0] + jnp.sum(x * x, axis=1, keepdims=True)
            acc[1] = acc[1] + dot(scaled, g_v[at, :])
            acc[2] = acc[2] + dot(scaled, u_v[at, :])

    expand(0)
    lax.fori_loop(0, nz, lambda d, carry: (relay(3, zat(d), False), carry)[1], 0)
    for d in range(1, nctx):
        expand(d)

    inverse = lax.rsqrt(acc[0] * (1.0 / (nctx * cols)) + EPS)
    gate, up = acc[1] * inverse, acc[2] * inverse
    got(w_all.at[other], wp_ss, wp_rs)
    weights = jnp.concatenate(
        [w_all[kk].reshape(half_rows, STAT) for kk in (k, other)], axis=0
    )
    weight = jnp.sum(jnp.where(iota((rows, STAT), 1) == e, weights, 0.0), axis=1, keepdims=True)
    active = jnp.where(weight > 0.0, gate / (1.0 + jnp.exp(-gate)) * up, 0.0).astype(BF16)
    local[3].wait()

    def contract(d):
        at = pl.ds(pl.multiple_of(ctx(d) * cols, cols), cols)
        out = dot(active, d_v[:, at]) * weight
        pf[d] = out[:half_rows]
        ps[d] = out[half_rows:].astype(BF16)
        pair(d).start()

    def pair(d):
        return send(ps.at[d], pr.at[d], p_ss.at[d], p_rs.at[d], dev(c, z, other))

    def across(d):
        return send(cs.at[d], cr.at[c], c_ss.at[d], c_rs.at[c], dev(ctx(d), z, k))

    def join(d):
        got(pr.at[d], p_ss.at[d], p_rs.at[d])
        both = pf[d] + pr[d].astype(F32)
        if d:
            cs[d] = both.astype(BF16)
            across(d).start()
        return both

    order = list(range(nctx - 1, -1, -1))
    contract(order[0])
    for before, now in zip(order[:-1], order[1:]):
        contract(now)
        join(before)
    total = join(0)
    for d in range(1, nctx):
        cc = ctx(d)
        got(cr.at[cc], c_ss.at[d], c_rs.at[cc])
        total = total + cr[cc].astype(F32)

    folded = fold(total)
    yf[...] = folded
    ys[...] = folded.astype(BF16)

    def send_y(zp):
        return send(ys.at[zp], yr.at[z], y_ss.at[zp], y_rs.at[z], dev(c, zp, k))

    z_loop(lambda zp: send_y(zp).start())
    for copy in att_copies:
        copy.wait_send()
    w2_copy.wait_send()
    wp_copy.wait_send()

    def drain_z(zp):
        send(w_all.at[k, z], w_all.at[k, z], w_ss.at[zp], w_rs.at[z], dev(c, zp, k)).wait_send()
        send(zs.at[zp], zr.at[z], z_ss.at[zp], z_rs.at[z], dev(c, zp, k)).wait_send()
        ag_z(zp).wait_send()

    z_loop(drain_z)

    def drain(zp, carry):
        for d in range(nctx):
            if d:
                ag_c(d, zp).wait_send()
            ag_p(ctx(d), zp).wait_send()
        return carry

    lax.fori_loop(0, nz, drain, 0)
    for d in range(nctx):
        pair(d).wait_send()
        if d:
            across(d).wait_send()
    result = hidden.astype(F32) + yf[z]

    def take_last(d, acc):
        zp = zat(d)
        got(yr.at[zp], y_ss.at[zp], y_rs.at[zp])
        return acc + yr[zp].astype(F32)

    result = lax.fori_loop(1, nz, take_last, result)
    out_ref[...] = jnp.concatenate([result[:row_dev], result[row_dev:]], axis=1)

    z_loop(lambda zp: send_y(zp).wait_send())


def local(
    nctx, nexp,
    queries, key_lift, value_lift, page_pool, fresh_latents, page_table, context_lengths, tree_parents,
    out_weight, residual, norm_gain, expert_ids, route_weights, gate_matrix, up_matrix, down_matrix,
):
    nz = nexp // 2
    rows = queries.shape[0]
    half_rows = rows // 2
    row_dev, cols = residual.shape
    half = cols // 2
    heads = key_lift.shape[0]
    width = heads * VD + STAT
    own_leaves, advance, ckv = fresh_latents.shape
    fresh_cols = -(-own_leaves * advance // 128) * 128
    gate, up, down = gate_matrix[0], up_matrix[0], down_matrix[0]
    dma = pltpu.SemaphoreType.DMA
    vm = pl.BlockSpec(memory_space=pltpu.VMEM)
    hbm = pl.BlockSpec(memory_space=pl.ANY)
    piece = (2 * row_dev, half)
    scratch = [
        pltpu.VMEM((page_pool.shape[0] * page_pool.shape[1] + fresh_cols, ckv), BF16),
        pltpu.VMEM((2, half_rows, width), BF16),
        pltpu.VMEM((2 * nctx, half_rows, width), BF16),
        pltpu.VMEM((2,) + out_weight.shape, BF16),
        pltpu.VMEM(gate.shape, BF16),
        pltpu.VMEM(up.shape, BF16),
        pltpu.VMEM(down.shape, BF16),
        pltpu.VMEM((2, nz, row_dev, STAT), F32),
        pltpu.VMEM((nz,) + piece, F32),
        pltpu.VMEM((nz,) + piece, BF16),
        pltpu.VMEM((nz,) + piece, BF16),
        pltpu.VMEM((nctx, 2, nz) + piece, BF16),
        pltpu.VMEM((nctx, half_rows, cols), F32),
        pltpu.VMEM((nctx, half_rows, cols), BF16),
        pltpu.VMEM((nctx, half_rows, cols), BF16),
        pltpu.VMEM((nctx, half_rows, cols), BF16),
        pltpu.VMEM((nctx, half_rows, cols), BF16),
        pltpu.VMEM((nz,) + piece, F32),
        pltpu.VMEM((nz,) + piece, BF16),
        pltpu.VMEM((nz,) + piece, BF16),
        dma((4,)),
        dma((2 * nctx,)), dma((2 * nctx,)),
        dma, dma,
        dma((nz,)), dma((nz,)),
        dma, dma,
        dma((nz,)), dma((nz,)),
        dma((nz,)), dma((nz,)),
        dma((nctx, nz)), dma((nctx, nz)),
        dma((nctx, nz)), dma((nctx, nz)),
        dma((nctx,)), dma((nctx,)),
        dma((nctx,)), dma((nctx,)),
        dma((nz,)), dma((nz,)),
    ]
    return pl.pallas_call(
        functools.partial(kernel, nctx, nexp, page_pool.shape[1], own_leaves),
        out_shape=jax.ShapeDtypeStruct((row_dev, cols), F32),
        in_specs=[vm] * 8 + [hbm] + [vm] * 4 + [hbm] * 3,
        out_specs=vm,
        scratch_shapes=scratch,
        compiler_params=pltpu.CompilerParams(
            collective_id=0, has_side_effects=True, vmem_limit_bytes=60 * 2**20
        ),
    )(
        queries, key_lift, value_lift, page_pool.reshape(-1, ckv), fresh_latents.reshape(-1, ckv), page_table,
        context_lengths.reshape(1, -1), tree_parents, out_weight, residual, norm_gain.reshape(1, -1),
        expert_ids, route_weights, gate, up, down,
    ).astype(BF16)


def solution(mesh):
    return jax.shard_map(
        functools.partial(local, mesh.shape["context"], mesh.shape["expert"]),
        mesh=mesh,
        in_specs=(
            P(None, "expert"),
            P("expert", None, None),
            P("expert", None, None),
            P("context", None, None),
            P("context", None, None),
            P(),
            P(),
            P(),
            P("expert", "context"),
            P("expert", "context"),
            P(),
            P("expert", None),
            P("expert", None),
            P("expert", None, "context"),
            P("expert", None, "context"),
            P("expert", "context", None),
        ),
        out_specs=P("expert", "context"),
        check_vma=False,
    )
```

```python
import functools

import jax
import jax.numpy as jnp
from jax import lax
from jax.experimental import pallas as pl
from jax.experimental.pallas import tpu as pltpu
from jax.sharding import PartitionSpec as P

LAT = 512
ROPE = 64
QK = 128
VD = 128
NEG = -(2.0**100)
EPS = 1e-06
F32 = jnp.float32
BF16 = jnp.bfloat16
MESH = pl.DeviceIdType.MESH
STAT = 128


def iota(shape, dim):
    return lax.broadcasted_iota(jnp.int32, shape, dim)


def dot(a, b):
    return jnp.dot(a, b, preferred_element_type=F32)


def dot_t(a, b):
    return lax.dot_general(a, b, (((1,), (1,)), ((), ())), preferred_element_type=F32)


def div(v, n):
    return jnp.right_shift(v, n.bit_length() - 1) if n & (n - 1) == 0 else v // n


def mod(v, n):
    return v & (n - 1) if n & (n - 1) == 0 else v % n


def spread(per_leaf, advance):
    leaves, n = per_leaf.shape
    return jnp.broadcast_to(per_leaf[:, None, :], (leaves, advance, n)).reshape(leaves * advance, n)


def masks(c, pt_ref, cl_ref, tp_ref, pool_keys, page_len, fresh_cols, own_leaves):
    leaves, slots = pt_ref.shape
    advance = tp_ref.shape[1]
    rows = leaves * advance
    lengths = jnp.sum(
        jnp.where(
            iota((leaves, leaves), 0) == iota((leaves, leaves), 1),
            jnp.broadcast_to(cl_ref[...].astype(F32), (leaves, leaves)),
            0.0,
        ),
        axis=1,
        keepdims=True,
    )
    remain = lengths - (iota((leaves, slots), 1) * page_len).astype(F32)
    table = pt_ref[...]
    lane = iota((leaves, pool_keys), 1)
    limit = jnp.zeros((leaves, pool_keys), F32)
    pages = pool_keys // page_len
    for p in range(pages):
        here = jnp.sum(jnp.where(table == c * pages + p, remain, 0.0), axis=1, keepdims=True)
        limit = jnp.where(div(lane, page_len) == p, here, limit)
    inside = jnp.where(mod(lane, page_len).astype(F32) < limit, 1.0, 0.0)
    pool_mask = spread(inside, advance)
    token = mod(iota((leaves, fresh_cols), 1), advance)
    parents = tp_ref[...]
    chains = [jnp.where(token == 0, 1.0, 0.0)]
    for t in range(1, advance):
        chain = jnp.where(token == t, 1.0, 0.0)
        for u in range(t):
            chain = jnp.where(parents[:, t : t + 1] == u, chain + chains[u], chain)
        chains.append(chain)
    row = iota((rows, fresh_cols), 0)
    col = iota((rows, fresh_cols), 1)
    linked = jnp.zeros((rows, fresh_cols), F32)
    for t in range(advance):
        linked = jnp.where(mod(row, advance) == t, spread(chains[t], advance), linked)
    own = (div(row, advance) == c * own_leaves + div(col, advance)) & (col < own_leaves * advance)
    fresh_mask = jnp.where(own, linked, 0.0)
    return jnp.concatenate([pool_mask, fresh_mask], axis=1) > 0.5


def kernel(
    nctx, nexp, page_len, own_leaves,
    q_hbm, kl_hbm, vl_hbm, pool_hbm, fresh_hbm, pt_hbm, cl_hbm, tp_hbm, ow_hbm, res_ref, gain_hbm, ids_hbm,
    rw_hbm, g_hbm, u_hbm, d_hbm, out_ref,
    q_ref, kl_ref, vl_ref, pt_ref, cl_ref, tp_ref, gain_ref, ids_ref, rw_ref,
    kf, att_send, att_recv, w2, g_v, u_v, d_v, w_all, zf, zs, zr, xg, pf, ps, pr, cs, cr, yf, ys, yr,
    loc, att_ss, att_rs, w2_ss, w2_rs, w_ss, w_rs, wp_ss, wp_rs, z_ss, z_rs, agz_ss, agz_rs, agc_ss, agc_rs,
    agp_ss, agp_rs, p_ss, p_rs, c_ss, c_rs, y_ss, y_rs,
):
    c = lax.axis_index("context")
    e = lax.axis_index("expert")
    k, z = e % 2, e // 2
    nz = nexp // 2
    rows = q_hbm.shape[0]
    half_rows = rows // 2
    heads = kl_hbm.shape[0]
    row_dev, cols = res_ref.shape
    half = cols // 2
    other = 1 - k

    near = [((c // 2 + d // 2) % (nctx // 2)) * 2 + (c + d) % 2 for d in range(nctx)]
    turn = 1 - 2 * (z // (nz // 2))

    def ctx(d):
        return near[d]

    def zat(d):
        return (z + turn * d + nz) % nz

    def dev(cc, zz, kk):
        return (cc, zz * 2 + kk)

    def send(src, dst, ss, rs, to):
        return pltpu.make_async_remote_copy(
            src_ref=src, dst_ref=dst, send_sem=ss, recv_sem=rs, device_id=to, device_id_type=MESH
        )

    def got(dst, ss, rs):
        send(dst, dst, ss, rs, dev(c, z, other)).wait_recv()

    def z_loop(body):
        lax.fori_loop(1, nz, lambda d, carry: (body(zat(d)), carry)[1], 0)

    barrier = pltpu.get_barrier_semaphore()
    for d in range(nctx):
        for kk in range(2):
            if d or kk:
                pl.semaphore_signal(
                    barrier, inc=1, device_id=dev(ctx(d), z, (k + kk) % 2), device_id_type=MESH
                )
    z_loop(lambda zp: pl.semaphore_signal(barrier, inc=1, device_id=dev(c, zp, k), device_id_type=MESH))

    pool_keys = pool_hbm.shape[0]
    fresh_keys = fresh_hbm.shape[0]
    fresh_cols = kf.shape[0] - pool_keys
    pairs = [
        (pt_hbm, pt_ref),
        (cl_hbm, cl_ref),
        (tp_hbm, tp_ref),
        (ids_hbm, ids_ref),
        (rw_hbm, rw_ref),
        (q_hbm, q_ref),
        (kl_hbm, kl_ref),
        (pool_hbm, kf.at[0:pool_keys, :]),
        (fresh_hbm, kf.at[pool_keys : pool_keys + fresh_keys, :]),
        (vl_hbm, vl_ref),
        (ow_hbm, w2.at[k]),
        (gain_hbm, gain_ref),
        (g_hbm, g_v),
        (u_hbm, u_v),
        (d_hbm, d_v),
    ]
    local = [pltpu.make_async_copy(src, dst, loc.at[i]) for i, (src, dst) in enumerate(pairs)]
    for copy in local:
        copy.start()
    if fresh_cols != fresh_keys:
        kf[pool_keys + fresh_keys :, :] = jnp.zeros((fresh_cols - fresh_keys, kf.shape[1]), BF16)
    for copy in local[:5]:
        copy.wait()

    lane_w = iota((row_dev, STAT), 1)
    dense = jnp.zeros((row_dev, STAT), F32)
    ids, rw = ids_ref[...], rw_ref[...]
    for t in range(ids.shape[1]):
        dense = jnp.where(lane_w == ids[:, t : t + 1], rw[:, t : t + 1], dense)
    w_all[k, z] = dense

    mask = masks(c, pt_ref, cl_ref, tp_ref, pool_keys, page_len, fresh_cols, own_leaves)
    for copy in local[5:9]:
        copy.wait()
    qf = q_ref[...].astype(F32)
    scale = (QK + ROPE) ** (-0.5)
    keys = kf[...]
    lat, rot = [], []
    for h in range(heads):
        at = h * (QK + ROPE)
        lat.append(dot(qf[:, at : at + QK].astype(BF16), kl_ref[h]).astype(BF16))
        rot.append(qf[:, at + QK : at + QK + ROPE].astype(BF16))
    scores = dot_t(jnp.concatenate(lat, axis=0), keys[:, :LAT])
    scores = (scores + dot_t(jnp.concatenate(rot, axis=0), keys[:, LAT:])) * scale
    scores = jnp.concatenate(
        [jnp.where(mask, scores[h * rows : (h + 1) * rows], NEG) for h in range(heads)], axis=0
    )
    top = jnp.max(scores, axis=1, keepdims=True).astype(BF16).astype(F32)
    weight = jnp.exp(scores - top)
    total = jnp.sum(weight, axis=1, keepdims=True)
    numer = dot(weight.astype(BF16), keys[:, :LAT]) / total
    local[9].wait()
    high = numer.astype(BF16)
    low = (numer - high.astype(F32)).astype(BF16)
    t_high = total.astype(BF16).astype(F32)
    parts = []
    lane_s = iota((rows, STAT), 1)
    stats = jnp.zeros((rows, STAT), F32)
    for h in range(heads):
        own = slice(h * rows, (h + 1) * rows)
        parts.append(dot(high[own], vl_ref[h]) + dot(low[own], vl_ref[h]))
        for i, value in enumerate((top, t_high, total - t_high)):
            stats = jnp.where(lane_s == 3 * h + i, value[own], stats)
    width = heads * VD + STAT
    message = jnp.concatenate(parts + [stats], axis=1).reshape(nz, 2, row_dev, width)
    for kk in range(2):
        att_send[kk] = message[:, kk].reshape(half_rows, width).astype(BF16)
    att_recv[c * 2 + k] = att_send[k]

    pl.semaphore_wait(barrier, 2 * nctx - 1 + nz - 1)
    att_copies = []
    for d in range(nctx - 1, -1, -1):
        for kk in range(2):
            if d or kk:
                to = (k + kk) % 2
                att_copies.append(
                    send(att_send.at[to], att_recv.at[c * 2 + k], att_ss.at[2 * d + kk], att_rs.at[c * 2 + k],
                         dev(ctx(d), z, to))
                )
                att_copies[-1].start()
    w2_copy = send(ow_hbm, w2.at[k], w2_ss, w2_rs, dev(c, z, other))
    w2_copy.start()
    z_loop(lambda zp: send(w_all.at[k, z], w_all.at[k, z], w_ss.at[zp], w_rs.at[z], dev(c, zp, k)).start())
    for d in range(nctx):
        for kk in range(2):
            if d or kk:
                slot = ctx(d) * 2 + (k + kk) % 2
                got(att_recv.at[slot], att_ss.at[0], att_rs.at[slot])

    merged = []
    for kk in range(2):
        held = [att_recv[cc * 2 + kk].astype(F32) for cc in range(nctx)]
        for h in range(heads):
            base = heads * VD + 3 * h
            tops = [v[:, base : base + 1] for v in held]
            best = functools.reduce(jnp.maximum, tops)
            shares = [
                (v[:, base + 1 : base + 2] + v[:, base + 2 : base + 3]) * jnp.exp(t - best)
                for v, t in zip(held, tops)
            ]
            whole = functools.reduce(jnp.add, shares)
            mixed = functools.reduce(
                jnp.add, [s * v[:, h * VD : (h + 1) * VD] for s, v in zip(shares, held)]
            )
            merged.append((mixed / whole).astype(BF16))
    local[10].wait()
    got(w2.at[other], w2_ss, w2_rs)
    span = heads
    projected = dot(jnp.concatenate(merged[:span], axis=1), w2[0]) + dot(
        jnp.concatenate(merged[span:], axis=1), w2[1]
    )

    def fold(v):
        v = v.reshape(-1, row_dev, cols)
        return jnp.concatenate([v[:, :, :half], v[:, :, half:]], axis=1)

    folded = fold(projected)
    zf[...] = folded
    zs[...] = folded.astype(BF16)
    z_loop(lambda zp: send(zs.at[zp], zr.at[z], z_ss.at[zp], z_rs.at[z], dev(c, zp, k)).start())
    state = zf[z] + fold(res_ref[...].astype(F32))[0]

    def take(d, acc):
        zp = zat(d)
        got(zr.at[zp], z_ss.at[zp], z_rs.at[zp])
        return acc + zr[zp].astype(F32)

    state = lax.fori_loop(1, nz, take, state)
    hidden = state.astype(BF16)
    xg[c, k, z] = hidden

    def ag_z(zp):
        return send(xg.at[c, k, z], xg.at[c, k, z], agz_ss.at[zp], agz_rs.at[z], dev(c, zp, k))

    def ag_c(d, zp):
        piece = xg.at[c, k, zp]
        return send(piece, piece, agc_ss.at[d, zp], agc_rs.at[c, zp], dev(ctx(d), z, k))

    def ag_p(cc, zp):
        piece = xg.at[cc, k, zp]
        return send(piece, piece, agp_ss.at[cc, zp], agp_rs.at[cc, zp], dev(c, z, other))

    z_loop(lambda zp: ag_z(zp).start())

    def onward(zp):
        for d in range(1, nctx - 1):
            ag_c(d, zp).start()
        ag_p(c, zp).start()

    def arrived(zp):
        got(xg.at[c, k, zp], agz_ss.at[zp], agz_rs.at[zp])
        onward(zp)

    onward(z)
    z_loop(arrived)
    ag_c(nctx - 1, z).start()
    z_loop(lambda zp: ag_c(nctx - 1, zp).start())

    def relay(d):
        def body(step, carry):
            zp = zat(step)
            got(xg.at[ctx(d), k, zp], agc_ss.at[0, zp], agc_rs.at[ctx(d), zp])
            ag_p(ctx(d), zp).start()
            return carry

        lax.fori_loop(0, nz, body, 0)

    z_loop(lambda zp: got(w_all.at[k, zp], w_ss.at[zp], w_rs.at[zp]))
    wp_copy = send(w_all.at[k], w_all.at[k], wp_ss, wp_rs, dev(c, z, other))
    wp_copy.start()

    for copy in local[11:14]:
        copy.wait()
    acc = [jnp.zeros((rows, 1), F32), jnp.zeros((rows, g_v.shape[1]), F32), jnp.zeros((rows, g_v.shape[1]), F32)]

    def expand(d):
        cc = ctx(d)

        def body(zp, carry):
            got(xg.at[cc, other, zp], agp_ss.at[cc, zp], agp_rs.at[cc, zp])
            return carry

        lax.fori_loop(0, nz, body, 0)
        both = [xg[cc, kk].astype(F32) for kk in (k, other)]
        for i in range(2):
            x = jnp.concatenate(
                [v[:, i * row_dev : (i + 1) * row_dev].reshape(half_rows, half) for v in both], axis=0
            )
            at = pl.ds(pl.multiple_of(cc * cols + i * half, half), half)
            scaled = (x * gain_ref[:, at]).astype(BF16)
            acc[0] = acc[0] + jnp.sum(x * x, axis=1, keepdims=True)
            acc[1] = acc[1] + dot(scaled, g_v[at, :])
            acc[2] = acc[2] + dot(scaled, u_v[at, :])

    relay(1)
    expand(0)
    for d in range(2, nctx):
        relay(d)
        expand(d - 1)
    expand(nctx - 1)

    inverse = lax.rsqrt(acc[0] * (1.0 / (nctx * cols)) + EPS)
    gate, up = acc[1] * inverse, acc[2] * inverse
    got(w_all.at[other], wp_ss, wp_rs)
    weights = jnp.concatenate(
        [w_all[kk].reshape(half_rows, STAT) for kk in (k, other)], axis=0
    )
    weight = jnp.sum(jnp.where(iota((rows, STAT), 1) == e, weights, 0.0), axis=1, keepdims=True)
    active = jnp.where(weight > 0.0, gate / (1.0 + jnp.exp(-gate)) * up, 0.0).astype(BF16)
    local[14].wait()

    def contract(d):
        at = pl.ds(pl.multiple_of(ctx(d) * cols, cols), cols)
        out = dot(active, d_v[:, at]) * weight
        pf[d] = out[:half_rows]
        ps[d] = out[half_rows:].astype(BF16)
        pair(d).start()

    def pair(d):
        return send(ps.at[d], pr.at[d], p_ss.at[d], p_rs.at[d], dev(c, z, other))

    def across(d):
        return send(cs.at[d], cr.at[c], c_ss.at[d], c_rs.at[c], dev(ctx(d), z, k))

    def join(d):
        got(pr.at[d], p_ss.at[d], p_rs.at[d])
        both = pf[d] + pr[d].astype(F32)
        if d:
            cs[d] = both.astype(BF16)
            across(d).start()
        return both

    order = list(range(nctx - 1, -1, -1))
    contract(order[0])
    for before, now in zip(order[:-1], order[1:]):
        contract(now)
        join(before)
    total = join(0)
    for d in range(1, nctx):
        cc = ctx(d)
        got(cr.at[cc], c_ss.at[d], c_rs.at[cc])
        total = total + cr[cc].astype(F32)

    folded = fold(total)
    yf[...] = folded
    ys[...] = folded.astype(BF16)

    def send_y(zp):
        return send(ys.at[zp], yr.at[z], y_ss.at[zp], y_rs.at[z], dev(c, zp, k))

    z_loop(lambda zp: send_y(zp).start())
    for copy in att_copies:
        copy.wait_send()
    w2_copy.wait_send()
    wp_copy.wait_send()

    def drain_z(zp):
        send(w_all.at[k, z], w_all.at[k, z], w_ss.at[zp], w_rs.at[z], dev(c, zp, k)).wait_send()
        send(zs.at[zp], zr.at[z], z_ss.at[zp], z_rs.at[z], dev(c, zp, k)).wait_send()
        ag_z(zp).wait_send()

    z_loop(drain_z)

    def drain(zp, carry):
        for d in range(nctx):
            if d:
                ag_c(d, zp).wait_send()
            ag_p(ctx(d), zp).wait_send()
        return carry

    lax.fori_loop(0, nz, drain, 0)
    for d in range(nctx):
        pair(d).wait_send()
        if d:
            across(d).wait_send()
    result = hidden.astype(F32) + yf[z]

    def take_last(d, acc):
        zp = zat(d)
        got(yr.at[zp], y_ss.at[zp], y_rs.at[zp])
        return acc + yr[zp].astype(F32)

    result = lax.fori_loop(1, nz, take_last, result)
    out_ref[...] = jnp.concatenate([result[:row_dev], result[row_dev:]], axis=1).astype(BF16)

    z_loop(lambda zp: send_y(zp).wait_send())


def local(
    nctx, nexp,
    queries, key_lift, value_lift, page_pool, fresh_latents, page_table, context_lengths, tree_parents,
    out_weight, residual, norm_gain, expert_ids, route_weights, gate_matrix, up_matrix, down_matrix,
):
    nz = nexp // 2
    rows = queries.shape[0]
    half_rows = rows // 2
    row_dev, cols = residual.shape
    half = cols // 2
    heads = key_lift.shape[0]
    width = heads * VD + STAT
    own_leaves, advance, ckv = fresh_latents.shape
    fresh_cols = -(-own_leaves * advance // 128) * 128
    gate, up, down = gate_matrix[0], up_matrix[0], down_matrix[0]
    lengths, gain = context_lengths.reshape(1, -1), norm_gain.reshape(1, -1)
    dma = pltpu.SemaphoreType.DMA
    vm = pl.BlockSpec(memory_space=pltpu.VMEM)
    hbm = pl.BlockSpec(memory_space=pl.ANY)
    piece = (2 * row_dev, half)
    scratch = [pltpu.VMEM(a.shape, a.dtype) for a in (
        queries, key_lift, value_lift, page_table, lengths, tree_parents, gain, expert_ids, route_weights
    )] + [
        pltpu.VMEM((page_pool.shape[0] * page_pool.shape[1] + fresh_cols, ckv), BF16),
        pltpu.VMEM((2, half_rows, width), BF16),
        pltpu.VMEM((2 * nctx, half_rows, width), BF16),
        pltpu.VMEM((2,) + out_weight.shape, BF16),
        pltpu.VMEM(gate.shape, BF16),
        pltpu.VMEM(up.shape, BF16),
        pltpu.VMEM(down.shape, BF16),
        pltpu.VMEM((2, nz, row_dev, STAT), F32),
        pltpu.VMEM((nz,) + piece, F32),
        pltpu.VMEM((nz,) + piece, BF16),
        pltpu.VMEM((nz,) + piece, BF16),
        pltpu.VMEM((nctx, 2, nz) + piece, BF16),
        pltpu.VMEM((nctx, half_rows, cols), F32),
        pltpu.VMEM((nctx, half_rows, cols), BF16),
        pltpu.VMEM((nctx, half_rows, cols), BF16),
        pltpu.VMEM((nctx, half_rows, cols), BF16),
        pltpu.VMEM((nctx, half_rows, cols), BF16),
        pltpu.VMEM((nz,) + piece, F32),
        pltpu.VMEM((nz,) + piece, BF16),
        pltpu.VMEM((nz,) + piece, BF16),
        dma((15,)),
        dma((2 * nctx,)), dma((2 * nctx,)),
        dma, dma,
        dma((nz,)), dma((nz,)),
        dma, dma,
        dma((nz,)), dma((nz,)),
        dma((nz,)), dma((nz,)),
        dma((nctx, nz)), dma((nctx, nz)),
        dma((nctx, nz)), dma((nctx, nz)),
        dma((nctx,)), dma((nctx,)),
        dma((nctx,)), dma((nctx,)),
        dma((nz,)), dma((nz,)),
    ]
    return pl.pallas_call(
        functools.partial(kernel, nctx, nexp, page_pool.shape[1], own_leaves),
        out_shape=jax.ShapeDtypeStruct((row_dev, cols), BF16),
        in_specs=[hbm] * 9 + [vm] + [hbm] * 6,
        out_specs=vm,
        scratch_shapes=scratch,
        compiler_params=pltpu.CompilerParams(
            collective_id=0, has_side_effects=True, vmem_limit_bytes=60 * 2**20
        ),
    )(
        queries, key_lift, value_lift, page_pool.reshape(-1, ckv), fresh_latents.reshape(-1, ckv), page_table,
        lengths, tree_parents, out_weight, residual, gain,
        expert_ids, route_weights, gate, up, down,
    )


def solution(mesh):
    return jax.shard_map(
        functools.partial(local, mesh.shape["context"], mesh.shape["expert"]),
        mesh=mesh,
        in_specs=(
            P(None, "expert"),
            P("expert", None, None),
            P("expert", None, None),
            P("context", None, None),
            P("context", None, None),
            P(),
            P(),
            P(),
            P("expert", "context"),
            P("expert", "context"),
            P(),
            P("expert", None),
            P("expert", None),
            P("expert", None, "context"),
            P("expert", None, "context"),
            P("expert", "context", None),
        ),
        out_specs=P("expert", "context"),
        check_vma=False,
    )
```

```python
import functools

import jax
import jax.numpy as jnp
from jax import lax
from jax.experimental import pallas as pl
from jax.experimental.pallas import tpu as pltpu
from jax.sharding import PartitionSpec as P

LAT = 512
ROPE = 64
QK = 128
VD = 128
NEG = -(2.0**100)
EPS = 1e-06
F32 = jnp.float32
BF16 = jnp.bfloat16
MESH = pl.DeviceIdType.MESH
STAT = 128


def iota(shape, dim):
    return lax.broadcasted_iota(jnp.int32, shape, dim)


def dot(a, b):
    return jnp.dot(a, b, preferred_element_type=F32)


def dot_t(a, b):
    return lax.dot_general(a, b, (((1,), (1,)), ((), ())), preferred_element_type=F32)


def div(v, n):
    return jnp.right_shift(v, n.bit_length() - 1) if n & (n - 1) == 0 else v // n


def mod(v, n):
    return v & (n - 1) if n & (n - 1) == 0 else v % n


def spread(per_leaf, advance):
    leaves, n = per_leaf.shape
    return jnp.broadcast_to(per_leaf[:, None, :], (leaves, advance, n)).reshape(leaves * advance, n)


def masks(c, pt_ref, cl_ref, tp_ref, pool_keys, page_len, fresh_cols, own_leaves):
    leaves, slots = pt_ref.shape
    advance = tp_ref.shape[1]
    rows = leaves * advance
    lengths = jnp.sum(
        jnp.where(
            iota((leaves, leaves), 0) == iota((leaves, leaves), 1),
            jnp.broadcast_to(cl_ref[...].astype(F32), (leaves, leaves)),
            0.0,
        ),
        axis=1,
        keepdims=True,
    )
    remain = lengths - (iota((leaves, slots), 1) * page_len).astype(F32)
    table = pt_ref[...]
    lane = iota((leaves, pool_keys), 1)
    limit = jnp.zeros((leaves, pool_keys), F32)
    pages = pool_keys // page_len
    for p in range(pages):
        here = jnp.sum(jnp.where(table == c * pages + p, remain, 0.0), axis=1, keepdims=True)
        limit = jnp.where(div(lane, page_len) == p, here, limit)
    inside = jnp.where(mod(lane, page_len).astype(F32) < limit, 1.0, 0.0)
    pool_mask = spread(inside, advance)
    token = mod(iota((leaves, fresh_cols), 1), advance)
    parents = tp_ref[...]
    chains = [jnp.where(token == 0, 1.0, 0.0)]
    for t in range(1, advance):
        chain = jnp.where(token == t, 1.0, 0.0)
        for u in range(t):
            chain = jnp.where(parents[:, t : t + 1] == u, chain + chains[u], chain)
        chains.append(chain)
    row = iota((rows, fresh_cols), 0)
    col = iota((rows, fresh_cols), 1)
    linked = jnp.zeros((rows, fresh_cols), F32)
    for t in range(advance):
        linked = jnp.where(mod(row, advance) == t, spread(chains[t], advance), linked)
    own = (div(row, advance) == c * own_leaves + div(col, advance)) & (col < own_leaves * advance)
    fresh_mask = jnp.where(own, linked, 0.0)
    return jnp.concatenate([pool_mask, fresh_mask], axis=1) > 0.5


def kernel(
    nctx, nexp, page_len, own_leaves,
    q_hbm, kl_hbm, vl_hbm, pool_hbm, fresh_hbm, pt_hbm, cl_hbm, tp_hbm, ow_hbm, res_ref, gain_hbm, ids_hbm,
    rw_hbm, g_hbm, u_hbm, d_hbm, out_ref,
    q_ref, kl_ref, vl_ref, pt_ref, cl_ref, tp_ref, gain_ref, ids_ref, rw_ref,
    kf, att_send, att_recv, w2, g_v, u_v, d_v, w_all, zf, zs, zr, xg, pf, ps, pr, cs, cr, yf, ys, yr, vf, vs, vr, ts, tr,
    loc, att_ss, att_rs, w2_ss, w2_rs, w_ss, w_rs, wp_ss, wp_rs, z_ss, z_rs, agz_ss, agz_rs, agc_ss, agc_rs,
    agp_ss, agp_rs, p_ss, p_rs, c_ss, c_rs, y_ss, y_rs, v_ss, v_rs, t_ss, t_rs,
):
    c = lax.axis_index("context")
    e = lax.axis_index("expert")
    k, z = e % 2, e // 2
    nz = nexp // 2
    rows = q_hbm.shape[0]
    half_rows = rows // 2
    heads = kl_hbm.shape[0]
    row_dev, cols = res_ref.shape
    half = cols // 2
    other = 1 - k

    near = [((c // 2 + d // 2) % (nctx // 2)) * 2 + (c + d) % 2 for d in range(nctx)]
    turn = 1 - 2 * (z // (nz // 2))

    def ctx(d):
        return near[d]

    def zat(d):
        return (z + turn * d + nz) % nz

    def dev(cc, zz, kk):
        return (cc, zz * 2 + kk)

    def send(src, dst, ss, rs, to):
        return pltpu.make_async_remote_copy(
            src_ref=src, dst_ref=dst, send_sem=ss, recv_sem=rs, device_id=to, device_id_type=MESH
        )

    def got(dst, ss, rs):
        send(dst, dst, ss, rs, dev(c, z, other)).wait_recv()

    def z_loop(body):
        lax.fori_loop(1, nz, lambda d, carry: (body(zat(d)), carry)[1], 0)

    barrier = pltpu.get_barrier_semaphore()
    for d in range(nctx):
        for kk in range(2):
            if d or kk:
                pl.semaphore_signal(
                    barrier, inc=1, device_id=dev(ctx(d), z, (k + kk) % 2), device_id_type=MESH
                )
    z_loop(lambda zp: pl.semaphore_signal(barrier, inc=1, device_id=dev(c, zp, k), device_id_type=MESH))

    pool_keys = pool_hbm.shape[0]
    fresh_keys = fresh_hbm.shape[0]
    fresh_cols = kf.shape[0] - pool_keys
    pairs = [
        (pt_hbm, pt_ref),
        (cl_hbm, cl_ref),
        (tp_hbm, tp_ref),
        (ids_hbm, ids_ref),
        (rw_hbm, rw_ref),
        (q_hbm, q_ref),
        (kl_hbm, kl_ref),
        (pool_hbm, kf.at[0:pool_keys, :]),
        (fresh_hbm, kf.at[pool_keys : pool_keys + fresh_keys, :]),
        (vl_hbm, vl_ref),
        (ow_hbm, w2.at[k]),
        (gain_hbm, gain_ref),
        (g_hbm, g_v),
        (u_hbm, u_v),
        (d_hbm, d_v),
    ]
    local = [pltpu.make_async_copy(src, dst, loc.at[i]) for i, (src, dst) in enumerate(pairs)]
    for copy in local[:10]:
        copy.start()
    if fresh_cols != fresh_keys:
        kf[pool_keys + fresh_keys :, :] = jnp.zeros((fresh_cols - fresh_keys, kf.shape[1]), BF16)
    for copy in local[:5]:
        copy.wait()

    lane_w = iota((row_dev, STAT), 1)
    dense = jnp.zeros((row_dev, STAT), F32)
    ids, rw = ids_ref[...], rw_ref[...]
    for t in range(ids.shape[1]):
        dense = jnp.where(lane_w == ids[:, t : t + 1], rw[:, t : t + 1], dense)
    w_all[k, z] = dense

    mask = masks(c, pt_ref, cl_ref, tp_ref, pool_keys, page_len, fresh_cols, own_leaves)
    for copy in local[5:10]:
        copy.wait()
    for copy in local[10:]:
        copy.start()
    qf = q_ref[...].astype(F32)
    scale = (QK + ROPE) ** (-0.5)
    keys = kf[...]
    lat, rot = [], []
    for h in range(heads):
        at = h * (QK + ROPE)
        lat.append(dot(qf[:, at : at + QK].astype(BF16), kl_ref[h]).astype(BF16))
        rot.append(qf[:, at + QK : at + QK + ROPE].astype(BF16))
    scores = dot_t(jnp.concatenate(lat, axis=0), keys[:, :LAT])
    scores = (scores + dot_t(jnp.concatenate(rot, axis=0), keys[:, LAT:])) * scale
    scores = jnp.concatenate(
        [jnp.where(mask, scores[h * rows : (h + 1) * rows], NEG) for h in range(heads)], axis=0
    )
    top = jnp.max(scores, axis=1, keepdims=True).astype(BF16).astype(F32)
    weight = jnp.exp(scores - top)
    total = jnp.sum(weight, axis=1, keepdims=True)
    numer = dot(weight.astype(BF16), keys[:, :LAT]) / total
    high = numer.astype(BF16)
    low = (numer - high.astype(F32)).astype(BF16)
    t_high = total.astype(BF16).astype(F32)
    parts = []
    lane_s = iota((rows, STAT), 1)
    stats = jnp.zeros((rows, STAT), F32)
    for h in range(heads):
        own = slice(h * rows, (h + 1) * rows)
        parts.append(dot(high[own], vl_ref[h]) + dot(low[own], vl_ref[h]))
        for i, value in enumerate((top, t_high, total - t_high)):
            stats = jnp.where(lane_s == 3 * h + i, value[own], stats)
    width = heads * VD + STAT
    message = jnp.concatenate(parts + [stats], axis=1).reshape(nz, 2, row_dev, width)
    for kk in range(2):
        att_send[kk] = message[:, kk].reshape(half_rows, width).astype(BF16)
    att_recv[c * 2 + k] = att_send[k]

    pl.semaphore_wait(barrier, 2 * nctx - 1 + nz - 1)
    att_copies = []
    for d in range(nctx - 1, -1, -1):
        for kk in range(2):
            if d or kk:
                to = (k + kk) % 2
                att_copies.append(
                    send(att_send.at[to], att_recv.at[c * 2 + k], att_ss.at[2 * d + kk], att_rs.at[c * 2 + k],
                         dev(ctx(d), z, to))
                )
                att_copies[-1].start()
    w2_copy = send(ow_hbm, w2.at[k], w2_ss, w2_rs, dev(c, z, other))
    w2_copy.start()
    z_loop(lambda zp: send(w_all.at[k, z], w_all.at[k, z], w_ss.at[zp], w_rs.at[z], dev(c, zp, k)).start())
    for d in range(nctx):
        for kk in range(2):
            if d or kk:
                slot = ctx(d) * 2 + (k + kk) % 2
                got(att_recv.at[slot], att_ss.at[0], att_rs.at[slot])

    merged = []
    for kk in range(2):
        held = [att_recv[cc * 2 + kk].astype(F32) for cc in range(nctx)]
        for h in range(heads):
            base = heads * VD + 3 * h
            tops = [v[:, base : base + 1] for v in held]
            best = functools.reduce(jnp.maximum, tops)
            shares = [
                (v[:, base + 1 : base + 2] + v[:, base + 2 : base + 3]) * jnp.exp(t - best)
                for v, t in zip(held, tops)
            ]
            whole = functools.reduce(jnp.add, shares)
            mixed = functools.reduce(
                jnp.add, [s * v[:, h * VD : (h + 1) * VD] for s, v in zip(shares, held)]
            )
            merged.append((mixed / whole).astype(BF16))
    local[10].wait()
    got(w2.at[other], w2_ss, w2_rs)
    span = heads
    projected = dot(jnp.concatenate(merged[:span], axis=1), w2[0]) + dot(
        jnp.concatenate(merged[span:], axis=1), w2[1]
    )

    def fold(v, count):
        v = v.reshape(-1, count, v.shape[-1])
        mid = v.shape[-1] // 2
        return jnp.concatenate([v[:, :, :mid], v[:, :, mid:]], axis=1)

    def unfold(v, count):
        return jnp.concatenate([v[:count], v[count:]], axis=1)

    folded = fold(projected, row_dev)
    zf[...] = folded
    zs[...] = folded.astype(BF16)
    z_loop(lambda zp: send(zs.at[zp], zr.at[z], z_ss.at[zp], z_rs.at[z], dev(c, zp, k)).start())
    state = zf[z] + fold(res_ref[...].astype(F32), row_dev)[0]

    def take(d, acc):
        zp = zat(d)
        got(zr.at[zp], z_ss.at[zp], z_rs.at[zp])
        return acc + zr[zp].astype(F32)

    state = lax.fori_loop(1, nz, take, state)
    hidden = state.astype(BF16)
    xg[c, k, z] = hidden

    def ag_z(zp):
        return send(xg.at[c, k, z], xg.at[c, k, z], agz_ss.at[zp], agz_rs.at[z], dev(c, zp, k))

    def ag_c(d, zp):
        piece = xg.at[c, k, zp]
        return send(piece, piece, agc_ss.at[d, zp], agc_rs.at[c, zp], dev(ctx(d), z, k))

    def ag_p(cc, zp):
        piece = xg.at[cc, k, zp]
        return send(piece, piece, agp_ss.at[cc, zp], agp_rs.at[cc, zp], dev(c, z, other))

    z_loop(lambda zp: ag_z(zp).start())

    def onward(zp):
        for d in range(1, nctx - 1):
            ag_c(d, zp).start()
        ag_p(c, zp).start()

    def arrived(zp):
        got(xg.at[c, k, zp], agz_ss.at[zp], agz_rs.at[zp])
        onward(zp)

    onward(z)
    z_loop(arrived)
    ag_c(nctx - 1, z).start()
    z_loop(lambda zp: ag_c(nctx - 1, zp).start())

    def relay(d):
        def body(step, carry):
            zp = zat(step)
            got(xg.at[ctx(d), k, zp], agc_ss.at[0, zp], agc_rs.at[ctx(d), zp])
            ag_p(ctx(d), zp).start()
            return carry

        lax.fori_loop(0, nz, body, 0)

    z_loop(lambda zp: got(w_all.at[k, zp], w_ss.at[zp], w_rs.at[zp]))
    wp_copy = send(w_all.at[k], w_all.at[k], wp_ss, wp_rs, dev(c, z, other))
    wp_copy.start()

    for copy in local[11:14]:
        copy.wait()
    acc = [jnp.zeros((rows, 1), F32), jnp.zeros((rows, g_v.shape[1]), F32), jnp.zeros((rows, g_v.shape[1]), F32)]

    def expand(d):
        cc = ctx(d)

        def body(zp, carry):
            got(xg.at[cc, other, zp], agp_ss.at[cc, zp], agp_rs.at[cc, zp])
            return carry

        lax.fori_loop(0, nz, body, 0)
        both = [xg[cc, kk].astype(F32) for kk in (k, other)]
        for i in range(2):
            x = jnp.concatenate(
                [v[:, i * row_dev : (i + 1) * row_dev].reshape(half_rows, half) for v in both], axis=0
            )
            at = pl.ds(pl.multiple_of(cc * cols + i * half, half), half)
            scaled = (x * gain_ref[:, at]).astype(BF16)
            acc[0] = acc[0] + jnp.sum(x * x, axis=1, keepdims=True)
            acc[1] = acc[1] + dot(scaled, g_v[at, :])
            acc[2] = acc[2] + dot(scaled, u_v[at, :])

    relay(1)
    expand(0)
    for d in range(2, nctx):
        relay(d)
        expand(d - 1)
    expand(nctx - 1)

    inverse = lax.rsqrt(acc[0] * (1.0 / (nctx * cols)) + EPS)
    gate, up = acc[1] * inverse, acc[2] * inverse
    got(w_all.at[other], wp_ss, wp_rs)
    weights = jnp.concatenate(
        [w_all[kk].reshape(half_rows, STAT) for kk in (k, other)], axis=0
    )
    weight = jnp.sum(jnp.where(iota((rows, STAT), 1) == e, weights, 0.0), axis=1, keepdims=True)
    active = jnp.where(weight > 0.0, gate / (1.0 + jnp.exp(-gate)) * up, 0.0).astype(BF16)
    local[14].wait()

    def contract(d):
        at = pl.ds(pl.multiple_of(ctx(d) * cols, cols), cols)
        out = dot(active, d_v[:, at]) * weight
        pf[d] = out[:half_rows]
        ps[d] = out[half_rows:].astype(BF16)
        pair(d).start()

    def pair(d):
        return send(ps.at[d], pr.at[d], p_ss.at[d], p_rs.at[d], dev(c, z, other))

    def across(d):
        return send(cs.at[d], cr.at[c], c_ss.at[d], c_rs.at[c], dev(ctx(d), z, k))

    def join(d):
        got(pr.at[d], p_ss.at[d], p_rs.at[d])
        both = pf[d] + pr[d].astype(F32)
        if d:
            cs[d] = both[:, :wide].astype(BF16)
            across(d).start()
        side.append(both[:, wide:].reshape(nz, row_dev, cols - wide))
        if len(side) % 2 == 0:
            g = len(side) // 2 - 1
            stack = jnp.concatenate(side[-2:], axis=1)
            vf[g] = stack
            vs[g] = stack.astype(BF16)
            z_loop(lambda zp: send_v(g, zp).start())
        return both[:, :wide]

    def send_v(g, zp):
        return send(vs.at[g, zp], vr.at[g, z], v_ss.at[g, zp], v_rs.at[g, z], dev(c, zp, k))

    def send_t(d):
        return send(ts.at[d], tr.at[c], t_ss.at[d], t_rs.at[c], dev(ctx(d), z, k))

    wide = cs.shape[2]
    side = []
    order = list(range(nctx - 1, -1, -1))
    contract(order[0])
    for before, now in zip(order[:-1], order[1:]):
        contract(now)
        join(before)
    total = join(0)
    for d in range(1, nctx):
        cc = ctx(d)
        got(cr.at[cc], c_ss.at[d], c_rs.at[cc])
        total = total + cr[cc].astype(F32)

    folded = fold(total, row_dev)
    yf[...] = folded
    ys[...] = folded.astype(BF16)

    def send_y(zp):
        return send(ys.at[zp], yr.at[z], y_ss.at[zp], y_rs.at[z], dev(c, zp, k))

    z_loop(lambda zp: send_y(zp).start())

    sides = [None] * nctx
    for g in range(nctx // 2):

        def take_v(d, acc, g=g):
            zp = zat(d)
            got(vr.at[g, zp], v_ss.at[g, zp], v_rs.at[g, zp])
            return acc + vr[g, zp].astype(F32)

        summed = lax.fori_loop(1, nz, take_v, vf[g, z])
        for i in range(2):
            d = order[2 * g + i]
            sides[d] = summed[i * row_dev : (i + 1) * row_dev]
            if d:
                ts[d] = fold(sides[d], row_dev)[0].astype(BF16)
                send_t(d).start()
    for copy in att_copies:
        copy.wait_send()
    w2_copy.wait_send()
    wp_copy.wait_send()

    def drain_z(zp):
        send(w_all.at[k, z], w_all.at[k, z], w_ss.at[zp], w_rs.at[z], dev(c, zp, k)).wait_send()
        send(zs.at[zp], zr.at[z], z_ss.at[zp], z_rs.at[z], dev(c, zp, k)).wait_send()
        ag_z(zp).wait_send()
        for g in range(nctx // 2):
            send_v(g, zp).wait_send()

    z_loop(drain_z)

    def drain(zp, carry):
        for d in range(nctx):
            if d:
                ag_c(d, zp).wait_send()
            ag_p(ctx(d), zp).wait_send()
        return carry

    lax.fori_loop(0, nz, drain, 0)
    for d in range(nctx):
        pair(d).wait_send()
        if d:
            across(d).wait_send()
    side_sum = sides[0]
    for d in range(1, nctx):
        got(tr.at[ctx(d)], t_ss.at[d], t_rs.at[ctx(d)])
        side_sum = side_sum + unfold(tr[ctx(d)].astype(F32), row_dev)

    def take_last(d, acc):
        zp = zat(d)
        got(yr.at[zp], y_ss.at[zp], y_rs.at[zp])
        return acc + yr[zp].astype(F32)

    main_sum = unfold(lax.fori_loop(1, nz, take_last, yf[z]), row_dev)
    result = unfold(hidden.astype(F32), row_dev) + jnp.concatenate([main_sum, side_sum], axis=1)
    out_ref[...] = result.astype(BF16)
    for d in range(1, nctx):
        send_t(d).wait_send()
    z_loop(lambda zp: send_y(zp).wait_send())


def local(
    nctx, nexp,
    queries, key_lift, value_lift, page_pool, fresh_latents, page_table, context_lengths, tree_parents,
    out_weight, residual, norm_gain, expert_ids, route_weights, gate_matrix, up_matrix, down_matrix,
):
    nz = nexp // 2
    rows = queries.shape[0]
    half_rows = rows // 2
    row_dev, cols = residual.shape
    half = cols // 2
    heads = key_lift.shape[0]
    width = heads * VD + STAT
    own_leaves, advance, ckv = fresh_latents.shape
    fresh_cols = -(-own_leaves * advance // 128) * 128
    gate, up, down = gate_matrix[0], up_matrix[0], down_matrix[0]
    lengths, gain = context_lengths.reshape(1, -1), norm_gain.reshape(1, -1)
    dma = pltpu.SemaphoreType.DMA
    vm = pl.BlockSpec(memory_space=pltpu.VMEM)
    hbm = pl.BlockSpec(memory_space=pl.ANY)
    piece = (2 * row_dev, half)
    rest = 2 * cols // 7 // 256 * 256
    wide = cols - rest
    scratch = [pltpu.VMEM(a.shape, a.dtype) for a in (
        queries, key_lift, value_lift, page_table, lengths, tree_parents, gain, expert_ids, route_weights
    )] + [
        pltpu.VMEM((page_pool.shape[0] * page_pool.shape[1] + fresh_cols, ckv), BF16),
        pltpu.VMEM((2, half_rows, width), BF16),
        pltpu.VMEM((2 * nctx, half_rows, width), BF16),
        pltpu.VMEM((2,) + out_weight.shape, BF16),
        pltpu.VMEM(gate.shape, BF16),
        pltpu.VMEM(up.shape, BF16),
        pltpu.VMEM(down.shape, BF16),
        pltpu.VMEM((2, nz, row_dev, STAT), F32),
        pltpu.VMEM((nz,) + piece, F32),
        pltpu.VMEM((nz,) + piece, BF16),
        pltpu.VMEM((nz,) + piece, BF16),
        pltpu.VMEM((nctx, 2, nz) + piece, BF16),
        pltpu.VMEM((nctx, half_rows, cols), F32),
        pltpu.VMEM((nctx, half_rows, cols), BF16),
        pltpu.VMEM((nctx, half_rows, cols), BF16),
        pltpu.VMEM((nctx, half_rows, wide), BF16),
        pltpu.VMEM((nctx, half_rows, wide), BF16),
        pltpu.VMEM((nz, 2 * row_dev, wide // 2), F32),
        pltpu.VMEM((nz, 2 * row_dev, wide // 2), BF16),
        pltpu.VMEM((nz, 2 * row_dev, wide // 2), BF16),
        pltpu.VMEM((nctx // 2, nz, 2 * row_dev, rest), F32),
        pltpu.VMEM((nctx // 2, nz, 2 * row_dev, rest), BF16),
        pltpu.VMEM((nctx // 2, nz, 2 * row_dev, rest), BF16),
        pltpu.VMEM((nctx, 2 * row_dev, rest // 2), BF16),
        pltpu.VMEM((nctx, 2 * row_dev, rest // 2), BF16),
        dma((15,)),
        dma((2 * nctx,)), dma((2 * nctx,)),
        dma, dma,
        dma((nz,)), dma((nz,)),
        dma, dma,
        dma((nz,)), dma((nz,)),
        dma((nz,)), dma((nz,)),
        dma((nctx, nz)), dma((nctx, nz)),
        dma((nctx, nz)), dma((nctx, nz)),
        dma((nctx,)), dma((nctx,)),
        dma((nctx,)), dma((nctx,)),
        dma((nz,)), dma((nz,)),
        dma((nctx // 2, nz)), dma((nctx // 2, nz)),
        dma((nctx,)), dma((nctx,)),
    ]
    return pl.pallas_call(
        functools.partial(kernel, nctx, nexp, page_pool.shape[1], own_leaves),
        out_shape=jax.ShapeDtypeStruct((row_dev, cols), BF16),
        in_specs=[hbm] * 9 + [vm] + [hbm] * 6,
        out_specs=vm,
        scratch_shapes=scratch,
        compiler_params=pltpu.CompilerParams(
            collective_id=0, has_side_effects=True, vmem_limit_bytes=60 * 2**20
        ),
    )(
        queries, key_lift, value_lift, page_pool.reshape(-1, ckv), fresh_latents.reshape(-1, ckv), page_table,
        lengths, tree_parents, out_weight, residual, gain,
        expert_ids, route_weights, gate, up, down,
    )


def solution(mesh):
    return jax.shard_map(
        functools.partial(local, mesh.shape["context"], mesh.shape["expert"]),
        mesh=mesh,
        in_specs=(
            P(None, "expert"),
            P("expert", None, None),
            P("expert", None, None),
            P("context", None, None),
            P("context", None, None),
            P(),
            P(),
            P(),
            P("expert", "context"),
            P("expert", "context"),
            P(),
            P("expert", None),
            P("expert", None),
            P("expert", None, "context"),
            P("expert", None, "context"),
            P("expert", "context", None),
        ),
        out_specs=P("expert", "context"),
        check_vma=False,
    )
```

```python
import functools

import jax
import jax.numpy as jnp
from jax import lax
from jax.experimental import pallas as pl
from jax.experimental.pallas import tpu as pltpu
from jax.sharding import PartitionSpec as P

LAT = 512
ROPE = 64
QK = 128
VD = 128
NEG = -(2.0**100)
EPS = 1e-06
F32 = jnp.float32
BF16 = jnp.bfloat16
MESH = pl.DeviceIdType.MESH
STAT = 128


def iota(shape, dim):
    return lax.broadcasted_iota(jnp.int32, shape, dim)


def dot(a, b):
    return jnp.dot(a, b, preferred_element_type=F32)


def dot_t(a, b):
    return lax.dot_general(a, b, (((1,), (1,)), ((), ())), preferred_element_type=F32)


def div(v, n):
    return jnp.right_shift(v, n.bit_length() - 1) if n & (n - 1) == 0 else v // n


def mod(v, n):
    return v & (n - 1) if n & (n - 1) == 0 else v % n


def spread(per_leaf, advance):
    leaves, n = per_leaf.shape
    return jnp.broadcast_to(per_leaf[:, None, :], (leaves, advance, n)).reshape(leaves * advance, n)


def masks(c, pt_ref, cl_ref, tp_ref, pool_keys, page_len, fresh_cols, own_leaves):
    leaves, slots = pt_ref.shape
    advance = tp_ref.shape[1]
    rows = leaves * advance
    lengths = jnp.sum(
        jnp.where(
            iota((leaves, leaves), 0) == iota((leaves, leaves), 1),
            jnp.broadcast_to(cl_ref[...].astype(F32), (leaves, leaves)),
            0.0,
        ),
        axis=1,
        keepdims=True,
    )
    remain = lengths - (iota((leaves, slots), 1) * page_len).astype(F32)
    table = pt_ref[...]
    lane = iota((leaves, pool_keys), 1)
    limit = jnp.zeros((leaves, pool_keys), F32)
    pages = pool_keys // page_len
    for p in range(pages):
        here = jnp.sum(jnp.where(table == c * pages + p, remain, 0.0), axis=1, keepdims=True)
        limit = jnp.where(div(lane, page_len) == p, here, limit)
    inside = jnp.where(mod(lane, page_len).astype(F32) < limit, 1.0, 0.0)
    pool_mask = spread(inside, advance)
    token = mod(iota((leaves, fresh_cols), 1), advance)
    parents = tp_ref[...]
    chains = [jnp.where(token == 0, 1.0, 0.0)]
    for t in range(1, advance):
        chain = jnp.where(token == t, 1.0, 0.0)
        for u in range(t):
            chain = jnp.where(parents[:, t : t + 1] == u, chain + chains[u], chain)
        chains.append(chain)
    row = iota((rows, fresh_cols), 0)
    col = iota((rows, fresh_cols), 1)
    linked = jnp.zeros((rows, fresh_cols), F32)
    for t in range(advance):
        linked = jnp.where(mod(row, advance) == t, spread(chains[t], advance), linked)
    own = (div(row, advance) == c * own_leaves + div(col, advance)) & (col < own_leaves * advance)
    fresh_mask = jnp.where(own, linked, 0.0)
    return jnp.concatenate([pool_mask, fresh_mask], axis=1) > 0.5


def kernel(
    nctx, nexp, page_len, own_leaves,
    q_hbm, kl_hbm, vl_hbm, pool_hbm, fresh_hbm, pt_hbm, cl_hbm, tp_hbm, ow_hbm, res_ref, gain_hbm, ids_hbm,
    rw_hbm, g_hbm, u_hbm, d_hbm, out_ref,
    q_ref, kl_ref, vl_ref, pt_ref, cl_ref, tp_ref, gain_ref, ids_ref, rw_ref,
    kf, att_send, att_recv, w2, g_v, u_v, d_v, w_all, zf, zs, zr, xg, pf, ps, pr, cs, cr, yf, ys, yr, vf, vs, vr, ts, tr,
    loc, att_ss, att_rs, w2_ss, w2_rs, w_ss, w_rs, wp_ss, wp_rs, z_ss, z_rs, agz_ss, agz_rs, agc_ss, agc_rs,
    agp_ss, agp_rs, p_ss, p_rs, c_ss, c_rs, y_ss, y_rs, v_ss, v_rs, t_ss, t_rs,
):
    c = lax.axis_index("context")
    e = lax.axis_index("expert")
    k, z = e % 2, e // 2
    nz = nexp // 2
    rows = q_hbm.shape[0]
    half_rows = rows // 2
    heads = kl_hbm.shape[0]
    row_dev, cols = res_ref.shape
    half = cols // 2
    other = 1 - k

    near = [((c // 2 + d // 2) % (nctx // 2)) * 2 + (c + d) % 2 for d in range(nctx)]
    turn = 1 - 2 * (z // (nz // 2))

    def ctx(d):
        return near[d]

    def zat(d):
        return (z + turn * d + nz) % nz

    def dev(cc, zz, kk):
        return (cc, zz * 2 + kk)

    def send(src, dst, ss, rs, to):
        return pltpu.make_async_remote_copy(
            src_ref=src, dst_ref=dst, send_sem=ss, recv_sem=rs, device_id=to, device_id_type=MESH
        )

    def got(dst, ss, rs):
        send(dst, dst, ss, rs, dev(c, z, other)).wait_recv()

    def z_loop(body):
        lax.fori_loop(1, nz, lambda d, carry: (body(zat(d)), carry)[1], 0)

    barrier = pltpu.get_barrier_semaphore()
    for d in range(nctx):
        for kk in range(2):
            if d or kk:
                pl.semaphore_signal(
                    barrier, inc=1, device_id=dev(ctx(d), z, (k + kk) % 2), device_id_type=MESH
                )
    z_loop(lambda zp: pl.semaphore_signal(barrier, inc=1, device_id=dev(c, zp, k), device_id_type=MESH))

    pool_keys = pool_hbm.shape[0]
    fresh_keys = fresh_hbm.shape[0]
    fresh_cols = kf.shape[0] - pool_keys
    pairs = [
        (pt_hbm, pt_ref),
        (cl_hbm, cl_ref),
        (tp_hbm, tp_ref),
        (ids_hbm, ids_ref),
        (rw_hbm, rw_ref),
        (q_hbm, q_ref),
        (kl_hbm, kl_ref),
        (pool_hbm, kf.at[0:pool_keys, :]),
        (fresh_hbm, kf.at[pool_keys : pool_keys + fresh_keys, :]),
        (vl_hbm, vl_ref),
        (ow_hbm, w2.at[k]),
        (gain_hbm, gain_ref),
        (g_hbm, g_v),
        (u_hbm, u_v),
        (d_hbm, d_v),
    ]
    local = [pltpu.make_async_copy(src, dst, loc.at[i]) for i, (src, dst) in enumerate(pairs)]
    for copy in local[:10]:
        copy.start()
    if fresh_cols != fresh_keys:
        kf[pool_keys + fresh_keys :, :] = jnp.zeros((fresh_cols - fresh_keys, kf.shape[1]), BF16)
    for copy in local[:5]:
        copy.wait()

    lane_w = iota((row_dev, STAT), 1)
    dense = jnp.zeros((row_dev, STAT), F32)
    ids, rw = ids_ref[...], rw_ref[...]
    for t in range(ids.shape[1]):
        dense = jnp.where(lane_w == ids[:, t : t + 1], rw[:, t : t + 1], dense)
    w_all[k, z] = dense

    mask = masks(c, pt_ref, cl_ref, tp_ref, pool_keys, page_len, fresh_cols, own_leaves)
    for copy in local[5:10]:
        copy.wait()
    for copy in local[10:]:
        copy.start()
    qf = q_ref[...].astype(F32)
    scale = (QK + ROPE) ** (-0.5)
    keys = kf[...]
    lat, rot = [], []
    for h in range(heads):
        at = h * (QK + ROPE)
        lat.append(dot(qf[:, at : at + QK].astype(BF16), kl_ref[h]).astype(BF16))
        rot.append(qf[:, at + QK : at + QK + ROPE].astype(BF16))
    scores = dot_t(jnp.concatenate(lat, axis=0), keys[:, :LAT])
    scores = (scores + dot_t(jnp.concatenate(rot, axis=0), keys[:, LAT:])) * scale
    scores = jnp.concatenate(
        [jnp.where(mask, scores[h * rows : (h + 1) * rows], NEG) for h in range(heads)], axis=0
    )
    top = jnp.max(scores, axis=1, keepdims=True).astype(BF16).astype(F32)
    weight = jnp.exp(scores - top)
    total = jnp.sum(weight, axis=1, keepdims=True)
    numer = dot(weight.astype(BF16), keys[:, :LAT]) / total
    high = numer.astype(BF16)
    low = (numer - high.astype(F32)).astype(BF16)
    t_high = total.astype(BF16).astype(F32)
    parts = []
    lane_s = iota((rows, STAT), 1)
    stats = jnp.zeros((rows, STAT), F32)
    for h in range(heads):
        own = slice(h * rows, (h + 1) * rows)
        parts.append(dot(high[own], vl_ref[h]) + dot(low[own], vl_ref[h]))
        for i, value in enumerate((top, t_high, total - t_high)):
            stats = jnp.where(lane_s == 3 * h + i, value[own], stats)
    width = heads * VD + STAT
    message = jnp.concatenate(parts + [stats], axis=1).reshape(nz, 2, row_dev, width)
    for kk in range(2):
        att_send[kk] = message[:, kk].reshape(half_rows, width).astype(BF16)
    att_recv[c * 2 + k] = att_send[k]

    pl.semaphore_wait(barrier, 2 * nctx - 1 + nz - 1)
    att_copies = []
    for d in range(nctx - 1, -1, -1):
        for kk in range(2):
            if d or kk:
                to = (k + kk) % 2
                att_copies.append(
                    send(att_send.at[to], att_recv.at[c * 2 + k], att_ss.at[2 * d + kk], att_rs.at[c * 2 + k],
                         dev(ctx(d), z, to))
                )
                att_copies[-1].start()
    w2_copy = send(ow_hbm, w2.at[k], w2_ss, w2_rs, dev(c, z, other))
    w2_copy.start()
    z_loop(lambda zp: send(w_all.at[k, z], w_all.at[k, z], w_ss.at[zp], w_rs.at[z], dev(c, zp, k)).start())
    for d in range(nctx):
        for kk in range(2):
            if d or kk:
                slot = ctx(d) * 2 + (k + kk) % 2
                got(att_recv.at[slot], att_ss.at[0], att_rs.at[slot])

    merged = []
    for kk in range(2):
        held = [att_recv[cc * 2 + kk].astype(F32) for cc in range(nctx)]
        for h in range(heads):
            base = heads * VD + 3 * h
            tops = [v[:, base : base + 1] for v in held]
            best = functools.reduce(jnp.maximum, tops)
            shares = [
                (v[:, base + 1 : base + 2] + v[:, base + 2 : base + 3]) * jnp.exp(t - best)
                for v, t in zip(held, tops)
            ]
            whole = functools.reduce(jnp.add, shares)
            mixed = functools.reduce(
                jnp.add, [s * v[:, h * VD : (h + 1) * VD] for s, v in zip(shares, held)]
            )
            merged.append((mixed / whole).astype(BF16))
    local[10].wait()
    got(w2.at[other], w2_ss, w2_rs)
    span = heads
    projected = dot(jnp.concatenate(merged[:span], axis=1), w2[0]) + dot(
        jnp.concatenate(merged[span:], axis=1), w2[1]
    )

    def fold(v, count):
        v = v.reshape(-1, count, v.shape[-1])
        mid = v.shape[-1] // 2
        return jnp.concatenate([v[:, :, :mid], v[:, :, mid:]], axis=1)

    def unfold(v, count):
        return jnp.concatenate([v[:count], v[count:]], axis=1)

    folded = fold(projected, row_dev)
    zf[...] = folded
    zs[...] = folded.astype(BF16)
    z_loop(lambda zp: send(zs.at[zp], zr.at[z], z_ss.at[zp], z_rs.at[z], dev(c, zp, k)).start())
    state = zf[z] + fold(res_ref[...].astype(F32), row_dev)[0]

    def take(d, acc):
        zp = zat(d)
        got(zr.at[zp], z_ss.at[zp], z_rs.at[zp])
        return acc + zr[zp].astype(F32)

    state = lax.fori_loop(1, nz, take, state)
    hidden = state.astype(BF16)
    xg[c, k, z] = hidden

    def ag_z(zp):
        return send(xg.at[c, k, z], xg.at[c, k, z], agz_ss.at[zp], agz_rs.at[z], dev(c, zp, k))

    def ag_c(d, zp):
        piece = xg.at[c, k, zp]
        return send(piece, piece, agc_ss.at[d, zp], agc_rs.at[c, zp], dev(ctx(d), z, k))

    def ag_p(cc, zp):
        piece = xg.at[cc, k, zp]
        return send(piece, piece, agp_ss.at[cc, zp], agp_rs.at[cc, zp], dev(c, z, other))

    z_loop(lambda zp: ag_z(zp).start())

    def onward(zp):
        ag_p(c, zp).start()
        for d in range(1, nctx):
            ag_c(d, zp).start()

    def arrived(zp):
        got(xg.at[c, k, zp], agz_ss.at[zp], agz_rs.at[zp])
        onward(zp)

    onward(z)
    z_loop(arrived)

    def relay(d):
        def body(step, carry):
            zp = zat(step)
            got(xg.at[ctx(d), k, zp], agc_ss.at[0, zp], agc_rs.at[ctx(d), zp])
            ag_p(ctx(d), zp).start()
            return carry

        lax.fori_loop(0, nz, body, 0)

    z_loop(lambda zp: got(w_all.at[k, zp], w_ss.at[zp], w_rs.at[zp]))
    wp_copy = send(w_all.at[k], w_all.at[k], wp_ss, wp_rs, dev(c, z, other))
    wp_copy.start()

    for copy in local[11:14]:
        copy.wait()
    acc = [jnp.zeros((rows, 1), F32), jnp.zeros((rows, g_v.shape[1]), F32), jnp.zeros((rows, g_v.shape[1]), F32)]

    def expand(d):
        cc = ctx(d)

        def body(zp, carry):
            got(xg.at[cc, other, zp], agp_ss.at[cc, zp], agp_rs.at[cc, zp])
            return carry

        lax.fori_loop(0, nz, body, 0)
        both = [xg[cc, kk].astype(F32) for kk in (k, other)]
        x = jnp.concatenate(
            [
                jnp.concatenate([v[:, i * row_dev : (i + 1) * row_dev].reshape(half_rows, half) for v in both], axis=0)
                for i in range(2)
            ],
            axis=1,
        )
        at = pl.ds(pl.multiple_of(cc * cols, cols), cols)
        scaled = (x * gain_ref[:, at]).astype(BF16)
        acc[0] = acc[0] + jnp.sum(x * x, axis=1, keepdims=True)
        acc[1] = acc[1] + dot(scaled, g_v[at, :])
        acc[2] = acc[2] + dot(scaled, u_v[at, :])

    expand(0)
    relay(1)
    for d in range(2, nctx):
        relay(d)
        expand(d - 1)
    expand(nctx - 1)

    inverse = lax.rsqrt(acc[0] * (1.0 / (nctx * cols)) + EPS)
    gate, up = acc[1] * inverse, acc[2] * inverse
    got(w_all.at[other], wp_ss, wp_rs)
    weights = jnp.concatenate(
        [w_all[kk].reshape(half_rows, STAT) for kk in (k, other)], axis=0
    )
    weight = jnp.sum(jnp.where(iota((rows, STAT), 1) == e, weights, 0.0), axis=1, keepdims=True)
    active = jnp.where(weight > 0.0, gate / (1.0 + jnp.exp(-gate)) * up, 0.0).astype(BF16)
    local[14].wait()

    def contract(d):
        at = pl.ds(pl.multiple_of(ctx(d) * cols, cols), cols)
        out = dot(active, d_v[:, at]) * weight
        pf[d] = out[:half_rows]
        ps[d] = out[half_rows:].astype(BF16)
        pair(d).start()

    def pair(d):
        return send(ps.at[d], pr.at[d], p_ss.at[d], p_rs.at[d], dev(c, z, other))

    def across(d):
        return send(cs.at[d], cr.at[c], c_ss.at[d], c_rs.at[c], dev(ctx(d), z, k))

    def join(d):
        got(pr.at[d], p_ss.at[d], p_rs.at[d])
        both = pf[d] + pr[d].astype(F32)
        if d:
            cs[d] = both[:, :wide].astype(BF16)
            across(d).start()
        side.append(both[:, wide:].reshape(nz, row_dev, cols - wide))
        if len(side) % 2 == 0:
            g = len(side) // 2 - 1
            stack = jnp.concatenate(side[-2:], axis=1)
            vf[g] = stack
            vs[g] = stack.astype(BF16)
            z_loop(lambda zp: send_v(g, zp).start())
        return both[:, :wide]

    def send_v(g, zp):
        return send(vs.at[g, zp], vr.at[g, z], v_ss.at[g, zp], v_rs.at[g, z], dev(c, zp, k))

    def send_t(d):
        return send(ts.at[d], tr.at[c], t_ss.at[d], t_rs.at[c], dev(ctx(d), z, k))

    wide = cs.shape[2]
    side = []
    order = list(range(nctx - 1, -1, -1))
    contract(order[0])
    for before, now in zip(order[:-1], order[1:]):
        contract(now)
        join(before)
    total = join(0)
    for d in range(1, nctx):
        cc = ctx(d)
        got(cr.at[cc], c_ss.at[d], c_rs.at[cc])
        total = total + cr[cc].astype(F32)

    folded = fold(total, row_dev)
    yf[...] = folded
    ys[...] = folded.astype(BF16)

    def send_y(zp):
        return send(ys.at[zp], yr.at[z], y_ss.at[zp], y_rs.at[z], dev(c, zp, k))

    z_loop(lambda zp: send_y(zp).start())

    sides = [None] * nctx
    for g in range(nctx // 2):

        def take_v(d, acc, g=g):
            zp = zat(d)
            got(vr.at[g, zp], v_ss.at[g, zp], v_rs.at[g, zp])
            return acc + vr[g, zp].astype(F32)

        summed = lax.fori_loop(1, nz, take_v, vf[g, z])
        for i in range(2):
            d = order[2 * g + i]
            sides[d] = summed[i * row_dev : (i + 1) * row_dev]
            if d:
                ts[d] = fold(sides[d], row_dev)[0].astype(BF16)
                send_t(d).start()
    for copy in att_copies:
        copy.wait_send()
    w2_copy.wait_send()
    wp_copy.wait_send()

    def drain_z(zp):
        send(w_all.at[k, z], w_all.at[k, z], w_ss.at[zp], w_rs.at[z], dev(c, zp, k)).wait_send()
        send(zs.at[zp], zr.at[z], z_ss.at[zp], z_rs.at[z], dev(c, zp, k)).wait_send()
        ag_z(zp).wait_send()
        for g in range(nctx // 2):
            send_v(g, zp).wait_send()

    z_loop(drain_z)

    def drain(zp, carry):
        for d in range(nctx):
            if d:
                ag_c(d, zp).wait_send()
            ag_p(ctx(d), zp).wait_send()
        return carry

    lax.fori_loop(0, nz, drain, 0)
    for d in range(nctx):
        pair(d).wait_send()
        if d:
            across(d).wait_send()
    side_sum = sides[0]
    for d in range(1, nctx):
        got(tr.at[ctx(d)], t_ss.at[d], t_rs.at[ctx(d)])
        side_sum = side_sum + unfold(tr[ctx(d)].astype(F32), row_dev)

    def take_last(d, acc):
        zp = zat(d)
        got(yr.at[zp], y_ss.at[zp], y_rs.at[zp])
        return acc + yr[zp].astype(F32)

    main_sum = unfold(lax.fori_loop(1, nz, take_last, yf[z]), row_dev)
    result = unfold(hidden.astype(F32), row_dev) + jnp.concatenate([main_sum, side_sum], axis=1)
    out_ref[...] = result.astype(BF16)
    for d in range(1, nctx):
        send_t(d).wait_send()
    z_loop(lambda zp: send_y(zp).wait_send())


def local(
    nctx, nexp,
    queries, key_lift, value_lift, page_pool, fresh_latents, page_table, context_lengths, tree_parents,
    out_weight, residual, norm_gain, expert_ids, route_weights, gate_matrix, up_matrix, down_matrix,
):
    nz = nexp // 2
    rows = queries.shape[0]
    half_rows = rows // 2
    row_dev, cols = residual.shape
    half = cols // 2
    heads = key_lift.shape[0]
    width = heads * VD + STAT
    own_leaves, advance, ckv = fresh_latents.shape
    fresh_cols = -(-own_leaves * advance // 128) * 128
    gate, up, down = gate_matrix[0], up_matrix[0], down_matrix[0]
    lengths, gain = context_lengths.reshape(1, -1), norm_gain.reshape(1, -1)
    dma = pltpu.SemaphoreType.DMA
    vm = pl.BlockSpec(memory_space=pltpu.VMEM)
    hbm = pl.BlockSpec(memory_space=pl.ANY)
    piece = (2 * row_dev, half)
    rest = 2 * cols // 7 // 256 * 256
    wide = cols - rest
    scratch = [pltpu.VMEM(a.shape, a.dtype) for a in (
        queries, key_lift, value_lift, page_table, lengths, tree_parents, gain, expert_ids, route_weights
    )] + [
        pltpu.VMEM((page_pool.shape[0] * page_pool.shape[1] + fresh_cols, ckv), BF16),
        pltpu.VMEM((2, half_rows, width), BF16),
        pltpu.VMEM((2 * nctx, half_rows, width), BF16),
        pltpu.VMEM((2,) + out_weight.shape, BF16),
        pltpu.VMEM(gate.shape, BF16),
        pltpu.VMEM(up.shape, BF16),
        pltpu.VMEM(down.shape, BF16),
        pltpu.VMEM((2, nz, row_dev, STAT), F32),
        pltpu.VMEM((nz,) + piece, F32),
        pltpu.VMEM((nz,) + piece, BF16),
        pltpu.VMEM((nz,) + piece, BF16),
        pltpu.VMEM((nctx, 2, nz) + piece, BF16),
        pltpu.VMEM((nctx, half_rows, cols), F32),
        pltpu.VMEM((nctx, half_rows, cols), BF16),
        pltpu.VMEM((nctx, half_rows, cols), BF16),
        pltpu.VMEM((nctx, half_rows, wide), BF16),
        pltpu.VMEM((nctx, half_rows, wide), BF16),
        pltpu.VMEM((nz, 2 * row_dev, wide // 2), F32),
        pltpu.VMEM((nz, 2 * row_dev, wide // 2), BF16),
        pltpu.VMEM((nz, 2 * row_dev, wide // 2), BF16),
        pltpu.VMEM((nctx // 2, nz, 2 * row_dev, rest), F32),
        pltpu.VMEM((nctx // 2, nz, 2 * row_dev, rest), BF16),
        pltpu.VMEM((nctx // 2, nz, 2 * row_dev, rest), BF16),
        pltpu.VMEM((nctx, 2 * row_dev, rest // 2), BF16),
        pltpu.VMEM((nctx, 2 * row_dev, rest // 2), BF16),
        dma((15,)),
        dma((2 * nctx,)), dma((2 * nctx,)),
        dma, dma,
        dma((nz,)), dma((nz,)),
        dma, dma,
        dma((nz,)), dma((nz,)),
        dma((nz,)), dma((nz,)),
        dma((nctx, nz)), dma((nctx, nz)),
        dma((nctx, nz)), dma((nctx, nz)),
        dma((nctx,)), dma((nctx,)),
        dma((nctx,)), dma((nctx,)),
        dma((nz,)), dma((nz,)),
        dma((nctx // 2, nz)), dma((nctx // 2, nz)),
        dma((nctx,)), dma((nctx,)),
    ]
    return pl.pallas_call(
        functools.partial(kernel, nctx, nexp, page_pool.shape[1], own_leaves),
        out_shape=jax.ShapeDtypeStruct((row_dev, cols), BF16),
        in_specs=[hbm] * 9 + [vm] + [hbm] * 6,
        out_specs=vm,
        scratch_shapes=scratch,
        compiler_params=pltpu.CompilerParams(
            collective_id=0, has_side_effects=True, vmem_limit_bytes=60 * 2**20
        ),
    )(
        queries, key_lift, value_lift, page_pool.reshape(-1, ckv), fresh_latents.reshape(-1, ckv), page_table,
        lengths, tree_parents, out_weight, residual, gain,
        expert_ids, route_weights, gate, up, down,
    )


def solution(mesh):
    return jax.shard_map(
        functools.partial(local, mesh.shape["context"], mesh.shape["expert"]),
        mesh=mesh,
        in_specs=(
            P(None, "expert"),
            P("expert", None, None),
            P("expert", None, None),
            P("context", None, None),
            P("context", None, None),
            P(),
            P(),
            P(),
            P("expert", "context"),
            P("expert", "context"),
            P(),
            P("expert", None),
            P("expert", None),
            P("expert", None, "context"),
            P("expert", None, "context"),
            P("expert", "context", None),
        ),
        out_specs=P("expert", "context"),
        check_vma=False,
    )
```

```python
import functools

import jax
import jax.numpy as jnp
from jax import lax
from jax.experimental import pallas as pl
from jax.experimental.pallas import tpu as pltpu
from jax.sharding import PartitionSpec as P

LAT = 512
ROPE = 64
QK = 128
VD = 128
NEG = -(2.0**100)
EPS = 1e-06
F32 = jnp.float32
BF16 = jnp.bfloat16
MESH = pl.DeviceIdType.MESH
STAT = 128


def iota(shape, dim):
    return lax.broadcasted_iota(jnp.int32, shape, dim)


def dot(a, b):
    return jnp.dot(a, b, preferred_element_type=F32)


def dot_t(a, b):
    return lax.dot_general(a, b, (((1,), (1,)), ((), ())), preferred_element_type=F32)


def div(v, n):
    return jnp.right_shift(v, n.bit_length() - 1) if n & (n - 1) == 0 else v // n


def mod(v, n):
    return v & (n - 1) if n & (n - 1) == 0 else v % n


def spread(per_leaf, advance):
    leaves, n = per_leaf.shape
    return jnp.broadcast_to(per_leaf[:, None, :], (leaves, advance, n)).reshape(leaves * advance, n)


def masks(c, pt_ref, cl_ref, tp_ref, pool_keys, page_len, fresh_cols, own_leaves):
    leaves, slots = pt_ref.shape
    advance = tp_ref.shape[1]
    rows = leaves * advance
    lengths = jnp.sum(
        jnp.where(
            iota((leaves, leaves), 0) == iota((leaves, leaves), 1),
            jnp.broadcast_to(cl_ref[...].astype(F32), (leaves, leaves)),
            0.0,
        ),
        axis=1,
        keepdims=True,
    )
    remain = lengths - (iota((leaves, slots), 1) * page_len).astype(F32)
    table = pt_ref[...]
    lane = iota((leaves, pool_keys), 1)
    limit = jnp.zeros((leaves, pool_keys), F32)
    pages = pool_keys // page_len
    for p in range(pages):
        here = jnp.sum(jnp.where(table == c * pages + p, remain, 0.0), axis=1, keepdims=True)
        limit = jnp.where(div(lane, page_len) == p, here, limit)
    inside = jnp.where(mod(lane, page_len).astype(F32) < limit, 1.0, 0.0)
    pool_mask = spread(inside, advance)
    token = mod(iota((leaves, fresh_cols), 1), advance)
    parents = tp_ref[...]
    chains = [jnp.where(token == 0, 1.0, 0.0)]
    for t in range(1, advance):
        chain = jnp.where(token == t, 1.0, 0.0)
        for u in range(t):
            chain = jnp.where(parents[:, t : t + 1] == u, chain + chains[u], chain)
        chains.append(chain)
    row = iota((rows, fresh_cols), 0)
    col = iota((rows, fresh_cols), 1)
    linked = jnp.zeros((rows, fresh_cols), F32)
    for t in range(advance):
        linked = jnp.where(mod(row, advance) == t, spread(chains[t], advance), linked)
    own = (div(row, advance) == c * own_leaves + div(col, advance)) & (col < own_leaves * advance)
    fresh_mask = jnp.where(own, linked, 0.0)
    return jnp.concatenate([pool_mask, fresh_mask], axis=1) > 0.5


def kernel(
    nctx, nexp, page_len, own_leaves,
    q_hbm, kl_hbm, vl_hbm, pool_hbm, fresh_hbm, pt_hbm, cl_hbm, tp_hbm, ow_hbm, res_ref, gain_hbm, ids_hbm,
    rw_hbm, g_hbm, u_hbm, d_hbm, out_ref,
    q_ref, kl_ref, vl_ref, pt_ref, cl_ref, tp_ref, gain_ref, ids_ref, rw_ref,
    kf, att_send, att_recv, w2, g_v, u_v, d_v, w_all, zf, zs, zr, xg, pf, ps, pr, cs, cr, yf, ys, yr, vf, vs, vr, ts, tr,
    loc, att_ss, att_rs, w2_ss, w2_rs, w_ss, w_rs, wp_ss, wp_rs, z_ss, z_rs, agz_ss, agz_rs, agc_ss, agc_rs,
    agp_ss, agp_rs, p_ss, p_rs, c_ss, c_rs, y_ss, y_rs, v_ss, v_rs, t_ss, t_rs,
):
    c = lax.axis_index("context")
    e = lax.axis_index("expert")
    k, z = e % 2, e // 2
    nz = nexp // 2
    rows = q_hbm.shape[0]
    half_rows = rows // 2
    heads = kl_hbm.shape[0]
    row_dev, cols = res_ref.shape
    half = cols // 2
    other = 1 - k

    near = [((c // 2 + d // 2) % (nctx // 2)) * 2 + (c + d) % 2 for d in range(nctx)]
    turn = 1 - 2 * (z // (nz // 2))

    def ctx(d):
        return near[d]

    def zat(d):
        return (z + turn * d + nz) % nz

    def dev(cc, zz, kk):
        return (cc, zz * 2 + kk)

    def send(src, dst, ss, rs, to):
        return pltpu.make_async_remote_copy(
            src_ref=src, dst_ref=dst, send_sem=ss, recv_sem=rs, device_id=to, device_id_type=MESH
        )

    def got(dst, ss, rs):
        send(dst, dst, ss, rs, dev(c, z, other)).wait_recv()

    def z_loop(body):
        lax.fori_loop(1, nz, lambda d, carry: (body(zat(d)), carry)[1], 0)

    def z_far(body):
        lax.fori_loop(1, nz, lambda d, carry: (body(zat(nz - d)), carry)[1], 0)

    barrier = pltpu.get_barrier_semaphore()
    for d in range(nctx):
        for kk in range(2):
            if d or kk:
                pl.semaphore_signal(
                    barrier, inc=1, device_id=dev(ctx(d), z, (k + kk) % 2), device_id_type=MESH
                )
    z_loop(lambda zp: pl.semaphore_signal(barrier, inc=1, device_id=dev(c, zp, k), device_id_type=MESH))

    pool_keys = pool_hbm.shape[0]
    fresh_keys = fresh_hbm.shape[0]
    fresh_cols = kf.shape[0] - pool_keys
    pairs = [
        (pt_hbm, pt_ref),
        (cl_hbm, cl_ref),
        (tp_hbm, tp_ref),
        (ids_hbm, ids_ref),
        (rw_hbm, rw_ref),
        (q_hbm, q_ref),
        (kl_hbm, kl_ref),
        (pool_hbm, kf.at[0:pool_keys, :]),
        (fresh_hbm, kf.at[pool_keys : pool_keys + fresh_keys, :]),
        (vl_hbm, vl_ref),
        (ow_hbm, w2.at[k]),
        (gain_hbm, gain_ref),
        (g_hbm, g_v),
        (u_hbm, u_v),
        (d_hbm, d_v),
    ]
    local = [pltpu.make_async_copy(src, dst, loc.at[i]) for i, (src, dst) in enumerate(pairs)]
    for copy in local[:10]:
        copy.start()
    if fresh_cols != fresh_keys:
        kf[pool_keys + fresh_keys :, :] = jnp.zeros((fresh_cols - fresh_keys, kf.shape[1]), BF16)
    for copy in local[:5]:
        copy.wait()

    lane_w = iota((row_dev, STAT), 1)
    dense = jnp.zeros((row_dev, STAT), F32)
    ids, rw = ids_ref[...], rw_ref[...]
    for t in range(ids.shape[1]):
        dense = jnp.where(lane_w == ids[:, t : t + 1], rw[:, t : t + 1], dense)
    w_all[k, z] = dense

    mask = masks(c, pt_ref, cl_ref, tp_ref, pool_keys, page_len, fresh_cols, own_leaves)
    for copy in local[5:10]:
        copy.wait()
    for copy in local[10:]:
        copy.start()
    qf = q_ref[...].astype(F32)
    scale = (QK + ROPE) ** (-0.5)
    keys = kf[...]
    lat, rot = [], []
    for h in range(heads):
        at = h * (QK + ROPE)
        lat.append(dot(qf[:, at : at + QK].astype(BF16), kl_ref[h]).astype(BF16))
        rot.append(qf[:, at + QK : at + QK + ROPE].astype(BF16))
    scores = dot_t(jnp.concatenate(lat, axis=0), keys[:, :LAT])
    scores = (scores + dot_t(jnp.concatenate(rot, axis=0), keys[:, LAT:])) * scale
    scores = jnp.concatenate(
        [jnp.where(mask, scores[h * rows : (h + 1) * rows], NEG) for h in range(heads)], axis=0
    )
    top = jnp.max(scores, axis=1, keepdims=True).astype(BF16).astype(F32)
    weight = jnp.exp(scores - top)
    total = jnp.sum(weight, axis=1, keepdims=True)
    numer = dot(weight.astype(BF16), keys[:, :LAT]) / total
    high = numer.astype(BF16)
    low = (numer - high.astype(F32)).astype(BF16)
    t_high = total.astype(BF16).astype(F32)
    parts = []
    lane_s = iota((rows, STAT), 1)
    stats = jnp.zeros((rows, STAT), F32)
    for h in range(heads):
        own = slice(h * rows, (h + 1) * rows)
        parts.append(dot(high[own], vl_ref[h]) + dot(low[own], vl_ref[h]))
        for i, value in enumerate((top, t_high, total - t_high)):
            stats = jnp.where(lane_s == 3 * h + i, value[own], stats)
    width = heads * VD + STAT
    message = jnp.concatenate(parts + [stats], axis=1).reshape(nz, 2, row_dev, width)
    for kk in range(2):
        att_send[kk] = message[:, kk].reshape(half_rows, width).astype(BF16)
    att_recv[c * 2 + k] = att_send[k]

    pl.semaphore_wait(barrier, 2 * nctx - 1 + nz - 1)
    att_copies = []
    for d in range(nctx - 1, -1, -1):
        for kk in range(2):
            if d or kk:
                to = (k + kk) % 2
                att_copies.append(
                    send(att_send.at[to], att_recv.at[c * 2 + k], att_ss.at[2 * d + kk], att_rs.at[c * 2 + k],
                         dev(ctx(d), z, to))
                )
                att_copies[-1].start()
    w2_copy = send(ow_hbm, w2.at[k], w2_ss, w2_rs, dev(c, z, other))
    w2_copy.start()
    z_loop(lambda zp: send(w_all.at[k, z], w_all.at[k, z], w_ss.at[zp], w_rs.at[z], dev(c, zp, k)).start())
    for d in range(nctx):
        for kk in range(2):
            if d or kk:
                slot = ctx(d) * 2 + (k + kk) % 2
                got(att_recv.at[slot], att_ss.at[0], att_rs.at[slot])

    merged = []
    for kk in range(2):
        held = [att_recv[cc * 2 + kk].astype(F32) for cc in range(nctx)]
        for h in range(heads):
            base = heads * VD + 3 * h
            tops = [v[:, base : base + 1] for v in held]
            best = functools.reduce(jnp.maximum, tops)
            shares = [
                (v[:, base + 1 : base + 2] + v[:, base + 2 : base + 3]) * jnp.exp(t - best)
                for v, t in zip(held, tops)
            ]
            whole = functools.reduce(jnp.add, shares)
            mixed = functools.reduce(
                jnp.add, [s * v[:, h * VD : (h + 1) * VD] for s, v in zip(shares, held)]
            )
            merged.append((mixed / whole).astype(BF16))
    local[10].wait()
    got(w2.at[other], w2_ss, w2_rs)
    span = heads
    projected = dot(jnp.concatenate(merged[:span], axis=1), w2[0]) + dot(
        jnp.concatenate(merged[span:], axis=1), w2[1]
    )

    def fold(v, count):
        v = v.reshape(-1, count, v.shape[-1])
        mid = v.shape[-1] // 2
        return jnp.concatenate([v[:, :, :mid], v[:, :, mid:]], axis=1)

    def unfold(v, count):
        return jnp.concatenate([v[:count], v[count:]], axis=1)

    folded = fold(projected, row_dev)
    zf[...] = folded
    zs[...] = folded.astype(BF16)
    z_far(lambda zp: send(zs.at[zp], zr.at[z], z_ss.at[zp], z_rs.at[z], dev(c, zp, k)).start())
    state = zf[z] + fold(res_ref[...].astype(F32), row_dev)[0]

    def take(d, acc):
        zp = zat(d)
        got(zr.at[zp], z_ss.at[zp], z_rs.at[zp])
        return acc + zr[zp].astype(F32)

    state = lax.fori_loop(1, nz, take, state)
    hidden = state.astype(BF16)
    xg[c, k, z] = hidden

    def ag_z(zp):
        return send(xg.at[c, k, z], xg.at[c, k, z], agz_ss.at[zp], agz_rs.at[z], dev(c, zp, k))

    def ag_c(d, zp):
        piece = xg.at[c, k, zp]
        return send(piece, piece, agc_ss.at[d, zp], agc_rs.at[c, zp], dev(ctx(d), z, k))

    def ag_p(cc, zp):
        piece = xg.at[cc, k, zp]
        return send(piece, piece, agp_ss.at[cc, zp], agp_rs.at[cc, zp], dev(c, z, other))

    z_far(lambda zp: ag_z(zp).start())

    def onward(zp):
        ag_p(c, zp).start()
        for d in range(1, nctx):
            ag_c(d, zp).start()

    def arrived(zp):
        got(xg.at[c, k, zp], agz_ss.at[zp], agz_rs.at[zp])
        onward(zp)

    onward(z)
    z_loop(arrived)

    def relay(d):
        def body(step, carry):
            zp = zat(step)
            got(xg.at[ctx(d), k, zp], agc_ss.at[0, zp], agc_rs.at[ctx(d), zp])
            ag_p(ctx(d), zp).start()
            return carry

        lax.fori_loop(0, nz, body, 0)

    z_loop(lambda zp: got(w_all.at[k, zp], w_ss.at[zp], w_rs.at[zp]))
    wp_copy = send(w_all.at[k], w_all.at[k], wp_ss, wp_rs, dev(c, z, other))
    wp_copy.start()

    for copy in local[11:14]:
        copy.wait()
    acc = [jnp.zeros((rows, 1), F32), jnp.zeros((rows, g_v.shape[1]), F32), jnp.zeros((rows, g_v.shape[1]), F32)]

    def expand(d):
        cc = ctx(d)

        def body(zp, carry):
            got(xg.at[cc, other, zp], agp_ss.at[cc, zp], agp_rs.at[cc, zp])
            return carry

        lax.fori_loop(0, nz, body, 0)
        both = [xg[cc, kk].astype(F32) for kk in (k, other)]
        x = jnp.concatenate(
            [
                jnp.concatenate([v[:, i * row_dev : (i + 1) * row_dev].reshape(half_rows, half) for v in both], axis=0)
                for i in range(2)
            ],
            axis=1,
        )
        at = pl.ds(pl.multiple_of(cc * cols, cols), cols)
        scaled = (x * gain_ref[:, at]).astype(BF16)
        acc[0] = acc[0] + jnp.sum(x * x, axis=1, keepdims=True)
        acc[1] = acc[1] + dot(scaled, g_v[at, :])
        acc[2] = acc[2] + dot(scaled, u_v[at, :])

    expand(0)
    relay(1)
    for d in range(2, nctx):
        relay(d)
        expand(d - 1)
    expand(nctx - 1)

    inverse = lax.rsqrt(acc[0] * (1.0 / (nctx * cols)) + EPS)
    gate, up = acc[1] * inverse, acc[2] * inverse
    got(w_all.at[other], wp_ss, wp_rs)
    weights = jnp.concatenate(
        [w_all[kk].reshape(half_rows, STAT) for kk in (k, other)], axis=0
    )
    weight = jnp.sum(jnp.where(iota((rows, STAT), 1) == e, weights, 0.0), axis=1, keepdims=True)
    active = jnp.where(weight > 0.0, gate / (1.0 + jnp.exp(-gate)) * up, 0.0).astype(BF16)
    local[14].wait()

    def contract(d):
        at = pl.ds(pl.multiple_of(ctx(d) * cols, cols), cols)
        out = dot(active, d_v[:, at]) * weight
        pf[d] = out[:half_rows]
        ps[d] = out[half_rows:].astype(BF16)
        pair(d).start()

    def pair(d):
        return send(ps.at[d], pr.at[d], p_ss.at[d], p_rs.at[d], dev(c, z, other))

    def across(d):
        return send(cs.at[d], cr.at[c], c_ss.at[d], c_rs.at[c], dev(ctx(d), z, k))

    def join(d):
        got(pr.at[d], p_ss.at[d], p_rs.at[d])
        both = pf[d] + pr[d].astype(F32)
        if d:
            cs[d] = both[:, :wide].astype(BF16)
            across(d).start()
        side.append(both[:, wide:].reshape(nz, row_dev, cols - wide))
        if len(side) % 2 == 0:
            g = len(side) // 2 - 1
            stack = jnp.concatenate(side[-2:], axis=1)
            vf[g] = stack
            vs[g] = stack.astype(BF16)
            z_far(lambda zp: send_v(g, zp).start())
        return both[:, :wide]

    def send_v(g, zp):
        return send(vs.at[g, zp], vr.at[g, z], v_ss.at[g, zp], v_rs.at[g, z], dev(c, zp, k))

    def send_t(d):
        return send(ts.at[d], tr.at[c], t_ss.at[d], t_rs.at[c], dev(ctx(d), z, k))

    wide = cs.shape[2]
    side = []
    order = list(range(nctx - 1, -1, -1))
    contract(order[0])
    for before, now in zip(order[:-1], order[1:]):
        contract(now)
        join(before)
    total = join(0)
    for d in range(1, nctx):
        cc = ctx(d)
        got(cr.at[cc], c_ss.at[d], c_rs.at[cc])
        total = total + cr[cc].astype(F32)

    folded = fold(total, row_dev)
    yf[...] = folded
    ys[...] = folded.astype(BF16)

    def send_y(zp):
        return send(ys.at[zp], yr.at[z], y_ss.at[zp], y_rs.at[z], dev(c, zp, k))

    z_far(lambda zp: send_y(zp).start())

    sides = [None] * nctx
    for g in range(nctx // 2):

        def take_v(d, acc, g=g):
            zp = zat(d)
            got(vr.at[g, zp], v_ss.at[g, zp], v_rs.at[g, zp])
            return acc + vr[g, zp].astype(F32)

        summed = lax.fori_loop(1, nz, take_v, vf[g, z])
        for i in range(2):
            d = order[2 * g + i]
            sides[d] = summed[i * row_dev : (i + 1) * row_dev]
            if d:
                ts[d] = fold(sides[d], row_dev)[0].astype(BF16)
                send_t(d).start()
    for copy in att_copies:
        copy.wait_send()
    w2_copy.wait_send()
    wp_copy.wait_send()

    def drain_z(zp):
        send(w_all.at[k, z], w_all.at[k, z], w_ss.at[zp], w_rs.at[z], dev(c, zp, k)).wait_send()
        send(zs.at[zp], zr.at[z], z_ss.at[zp], z_rs.at[z], dev(c, zp, k)).wait_send()
        ag_z(zp).wait_send()
        for g in range(nctx // 2):
            send_v(g, zp).wait_send()

    z_loop(drain_z)

    def drain(zp, carry):
        for d in range(nctx):
            if d:
                ag_c(d, zp).wait_send()
            ag_p(ctx(d), zp).wait_send()
        return carry

    lax.fori_loop(0, nz, drain, 0)
    for d in range(nctx):
        pair(d).wait_send()
        if d:
            across(d).wait_send()
    side_sum = sides[0]
    for d in range(1, nctx):
        got(tr.at[ctx(d)], t_ss.at[d], t_rs.at[ctx(d)])
        side_sum = side_sum + unfold(tr[ctx(d)].astype(F32), row_dev)

    def take_last(d, acc):
        zp = zat(d)
        got(yr.at[zp], y_ss.at[zp], y_rs.at[zp])
        return acc + yr[zp].astype(F32)

    main_sum = unfold(lax.fori_loop(1, nz, take_last, yf[z]), row_dev)
    result = unfold(hidden.astype(F32), row_dev) + jnp.concatenate([main_sum, side_sum], axis=1)
    out_ref[...] = result.astype(BF16)
    for d in range(1, nctx):
        send_t(d).wait_send()
    z_loop(lambda zp: send_y(zp).wait_send())


def local(
    nctx, nexp,
    queries, key_lift, value_lift, page_pool, fresh_latents, page_table, context_lengths, tree_parents,
    out_weight, residual, norm_gain, expert_ids, route_weights, gate_matrix, up_matrix, down_matrix,
):
    nz = nexp // 2
    rows = queries.shape[0]
    half_rows = rows // 2
    row_dev, cols = residual.shape
    half = cols // 2
    heads = key_lift.shape[0]
    width = heads * VD + STAT
    own_leaves, advance, ckv = fresh_latents.shape
    fresh_cols = -(-own_leaves * advance // 128) * 128
    gate, up, down = gate_matrix[0], up_matrix[0], down_matrix[0]
    lengths, gain = context_lengths.reshape(1, -1), norm_gain.reshape(1, -1)
    dma = pltpu.SemaphoreType.DMA
    vm = pl.BlockSpec(memory_space=pltpu.VMEM)
    hbm = pl.BlockSpec(memory_space=pl.ANY)
    piece = (2 * row_dev, half)
    rest = 2 * cols // 7 // 256 * 256
    wide = cols - rest
    scratch = [pltpu.VMEM(a.shape, a.dtype) for a in (
        queries, key_lift, value_lift, page_table, lengths, tree_parents, gain, expert_ids, route_weights
    )] + [
        pltpu.VMEM((page_pool.shape[0] * page_pool.shape[1] + fresh_cols, ckv), BF16),
        pltpu.VMEM((2, half_rows, width), BF16),
        pltpu.VMEM((2 * nctx, half_rows, width), BF16),
        pltpu.VMEM((2,) + out_weight.shape, BF16),
        pltpu.VMEM(gate.shape, BF16),
        pltpu.VMEM(up.shape, BF16),
        pltpu.VMEM(down.shape, BF16),
        pltpu.VMEM((2, nz, row_dev, STAT), F32),
        pltpu.VMEM((nz,) + piece, F32),
        pltpu.VMEM((nz,) + piece, BF16),
        pltpu.VMEM((nz,) + piece, BF16),
        pltpu.VMEM((nctx, 2, nz) + piece, BF16),
        pltpu.VMEM((nctx, half_rows, cols), F32),
        pltpu.VMEM((nctx, half_rows, cols), BF16),
        pltpu.VMEM((nctx, half_rows, cols), BF16),
        pltpu.VMEM((nctx, half_rows, wide), BF16),
        pltpu.VMEM((nctx, half_rows, wide), BF16),
        pltpu.VMEM((nz, 2 * row_dev, wide // 2), F32),
        pltpu.VMEM((nz, 2 * row_dev, wide // 2), BF16),
        pltpu.VMEM((nz, 2 * row_dev, wide // 2), BF16),
        pltpu.VMEM((nctx // 2, nz, 2 * row_dev, rest), F32),
        pltpu.VMEM((nctx // 2, nz, 2 * row_dev, rest), BF16),
        pltpu.VMEM((nctx // 2, nz, 2 * row_dev, rest), BF16),
        pltpu.VMEM((nctx, 2 * row_dev, rest // 2), BF16),
        pltpu.VMEM((nctx, 2 * row_dev, rest // 2), BF16),
        dma((15,)),
        dma((2 * nctx,)), dma((2 * nctx,)),
        dma, dma,
        dma((nz,)), dma((nz,)),
        dma, dma,
        dma((nz,)), dma((nz,)),
        dma((nz,)), dma((nz,)),
        dma((nctx, nz)), dma((nctx, nz)),
        dma((nctx, nz)), dma((nctx, nz)),
        dma((nctx,)), dma((nctx,)),
        dma((nctx,)), dma((nctx,)),
        dma((nz,)), dma((nz,)),
        dma((nctx // 2, nz)), dma((nctx // 2, nz)),
        dma((nctx,)), dma((nctx,)),
    ]
    return pl.pallas_call(
        functools.partial(kernel, nctx, nexp, page_pool.shape[1], own_leaves),
        out_shape=jax.ShapeDtypeStruct((row_dev, cols), BF16),
        in_specs=[hbm] * 9 + [vm] + [hbm] * 6,
        out_specs=vm,
        scratch_shapes=scratch,
        compiler_params=pltpu.CompilerParams(
            collective_id=0, has_side_effects=True, vmem_limit_bytes=min(60, 48 + rows // 16) * 2**20
        ),
    )(
        queries, key_lift, value_lift, page_pool.reshape(-1, ckv), fresh_latents.reshape(-1, ckv), page_table,
        lengths, tree_parents, out_weight, residual, gain,
        expert_ids, route_weights, gate, up, down,
    )


def solution(mesh):
    return jax.shard_map(
        functools.partial(local, mesh.shape["context"], mesh.shape["expert"]),
        mesh=mesh,
        in_specs=(
            P(None, "expert"),
            P("expert", None, None),
            P("expert", None, None),
            P("context", None, None),
            P("context", None, None),
            P(),
            P(),
            P(),
            P("expert", "context"),
            P("expert", "context"),
            P(),
            P("expert", None),
            P("expert", None),
            P("expert", None, "context"),
            P("expert", None, "context"),
            P("expert", "context", None),
        ),
        out_specs=P("expert", "context"),
        check_vma=False,
    )
```
